32 devices in a mesh: box: 16 (over z, y, core), mc: 2 (over x).
Axes of the slice: x: 2, y: 2, z: 4, core: 2. Of those that a mesh axis runs over, the one named last changes fastest.
Arguments:
- base_operator: float32 [16384, 1024], P('box')
- exterior_values: float32 [12288, 128], P('box'), may hold values from -6 to 6
- wire_label: int32 [16, 1024], P('box'), may hold values from 0 to 63, as said below
- wire_material: int32 [64], replicated, may hold values from 0 to 7
- permittivity: float32 [16], P('mc'), parts along dimension 0, may hold values from 1 to 10
- morton_slot: int32 [16], replicated, may hold values from 0 to 15, each once
Outputs:
- merged_rows: float32 [24576, 1536], P(('mc', 'box')), parts along dimension 0
- interface_values: float32 [8192, 128], P(('mc', 'box')), parts along dimension 0
- exterior_flux: float32 [24576, 128], P(('mc', 'box')), parts along dimension 0
The draws below stay inside these ranges and needn't reach their ends.
There are 2 independent parts, one for each index of `mc`. The reference program is written for one: setup_inputs(seed, part) draws one part's arguments, and reference() takes and returns one part's arrays. A program takes and returns all parts, laid end to end along the dimension named above; an argument that names none is the same for every part. Nothing has to cross between parts.
Inputs may be any that keep to these rules, and one draw needn't show every extreme that they name: `wire_label`: along each box's 4 * 256 boundary nodes the labels come in runs of equal wire, each run a whole number of aligned groups of 2 nodes.
All inputs are finite; a program needn't handle non-finite values.
Results may differ from the reference program's by a relative error of at most 0.00014.
Values sent between devices are 32-bit elements; how exact they have to be, the bound alone decides.
A program may use at most 64 MiB of HBM per device.

```python
import math
import jax
import jax.numpy as jnp
from jax import lax

F = 256
R = 128
WIRES = 64
LEVELS = 8
BOXES = 16


def draw_base_operator(key, part):
    nodes = 4 * F
    entries = jax.random.normal(key, (BOXES, nodes, nodes), jnp.float32)
    entries = entries / jnp.sqrt(jnp.float32(nodes))
    symmetric = 0.5 * (entries + jnp.swapaxes(entries, 1, 2))
    identity = jnp.eye(nodes, dtype=jnp.float32)
    return (symmetric + 2.5 * identity[None, :, :]).reshape(BOXES * nodes, nodes)


def draw_wire_label(key, part):
    groups = 2 * F
    start_key = jax.random.fold_in(key, 11)
    wire_key = jax.random.fold_in(key, 23)
    starts = (jax.random.randint(start_key, (BOXES, groups), 0, 4) == 0).astype(jnp.int32)
    starts = starts.at[:, 0].set(1)
    run_index = jnp.cumsum(starts, axis=1) - 1
    run_wire = jax.random.randint(wire_key, (BOXES, groups), 0, WIRES)
    group_wire = jnp.take_along_axis(run_wire, run_index.astype(jnp.int32), axis=1)
    return jnp.repeat(group_wire, 2, axis=1).astype(jnp.int32)


def set_ends(values, stream_key, smallest, largest):
    longest = values.shape.index(max(values.shape))
    spots = []
    for shift in (0, 1):
        where = [jax.random.randint(jax.random.fold_in(stream_key, axis), (), 0, length) for axis, length in enumerate(values.shape)]
        where[longest] = (where[longest] + shift) % values.shape[longest]
        spots.append(tuple(where))
    return values.at[spots[0]].set(smallest).at[spots[1]].set(largest)


def shard_levels(stream_key, shape, pieces, smallest, largest):
    level = 1.0
    for axis_at, blocks in pieces:
        heights = jax.random.uniform(jax.random.fold_in(jax.random.fold_in(stream_key, 6), axis_at), (blocks,), jnp.float32, smallest / len(pieces), largest / len(pieces))
        level = level * jnp.repeat(jnp.exp(heights), shape[axis_at] // blocks).reshape((-1,) + (1,) * (len(shape) - 1 - axis_at))
    return level


def bell_draw(stream_key, dims, deviation, limit, pieces=(), kind=jnp.bfloat16):
    drawn = deviation * jax.random.normal(stream_key, dims, jnp.float32)
    if pieces:
        drawn = drawn * shard_levels(stream_key, dims, pieces, -0.22, 0.18)
    return jnp.clip(drawn, -limit, limit).astype(kind)


def setup_inputs(seed: int = 0, part: int = 0) -> dict:
    splits = jax.random.split(jax.random.key(seed), 7)
    part_keys = jax.random.split(jax.random.fold_in(splits[6], part), 7)
    return {
        "base_operator": draw_base_operator(jax.random.fold_in(splits[6], 71), part),
        "exterior_values": bell_draw(splits[1], (BOXES * 3 * F, R), 1.0, 6.0, ((0, 16),), jnp.float32),
        "wire_label": draw_wire_label(jax.random.fold_in(splits[6], 71), part),
        "wire_material": set_ends(jax.random.randint(splits[3], (WIRES,), 0, LEVELS), jax.random.fold_in(splits[3], 1), 0, LEVELS - 1).astype(jnp.int32),
        "permittivity": jnp.clip(jnp.exp(jax.random.uniform(part_keys[4], (LEVELS,), jnp.float32, math.log(1.0), math.log(10.0))), 1.0, 10.0),
        "morton_slot": jax.random.permutation(splits[5], BOXES).astype(jnp.int32),
    }


def reference(base_operator, exterior_values, wire_label, wire_material, permittivity, morton_slot):
    face = base_operator.shape[1] // 4
    outer = 3 * face
    highest = lax.Precision.HIGHEST
    operators = base_operator.reshape(BOXES, 4 * face, 4 * face)
    values = exterior_values.reshape(BOXES, outer, exterior_values.shape[1])
    scales = jnp.sqrt(permittivity[wire_material][wire_label])
    inverse = jnp.zeros((BOXES,), jnp.int32).at[morton_slot].set(jnp.arange(BOXES, dtype=jnp.int32))
    partner = inverse[jnp.bitwise_xor(morton_slot, 1)]

    def one_box(index):
        own = operators[index] * scales[index][:, None] * scales[index][None, :]
        other_index = partner[index]
        other = operators[other_index][outer:] * scales[other_index][outer:, None] * scales[other_index][None, :]
        product = jnp.dot(own[outer:, :outer], values[index], precision=highest)
        product = product + jnp.dot(other[:, :outer], values[other_index], precision=highest)
        schur = own[outer:, outer:] + other[:, outer:]
        factor = jnp.linalg.cholesky(schur)
        stacked = jnp.concatenate([own[outer:, :outer], other[:, :outer], product], axis=1)
        solved = jax.scipy.linalg.cho_solve((factor, True), stacked)
        left = own[:outer, :outer] - jnp.dot(own[:outer, outer:], solved[:, :outer], precision=highest)
        right = -jnp.dot(own[:outer, outer:], solved[:, outer:2 * outer], precision=highest)
        interface = -solved[:, 2 * outer:]
        flux = jnp.dot(own[:outer, :outer], values[index], precision=highest) + jnp.dot(own[:outer, outer:], interface, precision=highest)
        return (jnp.concatenate([left, right], axis=1), interface, flux)
    merged, interface, flux = lax.map(one_box, jnp.arange(BOXES, dtype=jnp.int32))
    return (merged.reshape(BOXES * outer, 2 * outer), interface.reshape(BOXES * face, -1), flux.reshape(BOXES * outer, -1))
```

```python
import functools

import jax
import jax.numpy as jnp
from jax import lax
from jax.experimental import pallas as pl
from jax.experimental.pallas import tpu as pltpu
from jax.sharding import PartitionSpec as P

F32 = jnp.float32
HIGHEST = lax.Precision.HIGHEST


def flatten_rows(items, boxes):
    return tuple((item.reshape(boxes, -1) for item in items))


def split(x):
    high = x.astype(jnp.bfloat16)
    low = (x - high.astype(F32)).astype(jnp.bfloat16)
    return high, low


def dot_split(a, b):
    (ah, al), (bh, bl) = a, b
    dot = functools.partial(jnp.dot, preferred_element_type=F32)
    return dot(ah, bh) + (dot(ah, bl) + dot(al, bh))


def dot3(a, b):
    return dot_split(split(a), split(b))


def column_of(row):
    return jnp.broadcast_to(row, (128, row.shape[1])).T


def widen(column, width):
    return jnp.concatenate([column] * (width // 128), axis=1)


def norm(x):
    return jnp.sqrt(jnp.sum(x * x))


def eye(n):
    row = lax.broadcasted_iota(jnp.int32, (n, n), 0)
    col = lax.broadcasted_iota(jnp.int32, (n, n), 1)
    return jnp.where(row == col, 1.0, 0.0).astype(F32)


def direct_inverse(s_ref, x_ref):
    n = s_ref.shape[0]
    x_ref[...] = s_ref[...]
    row_id = lax.broadcasted_iota(jnp.int32, (n, n), 0)
    col_id = lax.broadcasted_iota(jnp.int32, (n, n), 1)

    def step(k, carry):
        x = x_ref[...]
        on_row = row_id == k
        on_col = col_id == k
        row = jnp.sum(jnp.where(on_row, x, 0.0), axis=0, keepdims=True)
        col = jnp.sum(jnp.where(on_col, x, 0.0), axis=1, keepdims=True)
        pivot = jnp.sum(jnp.where(on_row & on_col, x, 0.0))
        scaled = row / pivot
        rest = x - col * scaled
        x = jnp.where(on_row, scaled, jnp.where(on_col, -col / pivot, rest))
        x_ref[...] = jnp.where(on_row & on_col, 1.0 / pivot, x)
        return carry

    lax.fori_loop(0, n, step, 0)


def invert(s_ref, x_ref, r_ref):
    s = s_ref[...]
    n = s.shape[0]
    unit = eye(n)
    alpha = n / jnp.sum(s * s)

    def begin(alpha):
        first = unit - alpha * s
        x_ref[...] = alpha * (unit + first)
        residual = dot3(first, first)
        r_ref[...] = residual
        return norm(residual)

    size = begin(alpha)

    def safe_start(_):
        return begin(1.0 / jnp.max(jnp.sum(jnp.abs(s), axis=0, keepdims=True)))

    size = lax.cond(size < 0.9, lambda size: size, safe_start, size)
    s_parts = split(s)

    def going(state):
        size, count = state
        return (size > 1e-2) & (count < 40)

    def improve(state):
        size, count = state
        x = x_ref[...]
        x = x + dot3(x, r_ref[...])
        x_ref[...] = x
        residual = unit - dot_split(s_parts, split(x))
        r_ref[...] = residual
        return norm(residual), count + 1

    size, _ = lax.while_loop(going, improve, (size, jnp.int32(0)))
    x = x_ref[...]
    x = x + dot3(x, r_ref[...])
    residual = unit - jnp.dot(s, x, precision=HIGHEST, preferred_element_type=F32)
    x_ref[...] = x + dot3(x, residual)
    converged = (size < 1e-2) & (norm(residual) < 1e-3)

    @pl.when(jnp.logical_not(converged))
    def _():
        direct_inverse(s_ref, x_ref)


def solve_kernel(
    rows_ref, face_ref, values_ref, scale_ref, other_ref, product_ref,
    merged_ref, interface_ref, flux_ref,
    high_ref, low_ref, value_high, value_low, s_ref, x_ref, r_ref, column_ref,
):
    face = face_ref.shape[0]
    outer = 3 * face
    step = pl.program_id(0)
    scale = scale_ref[...]

    @pl.when(step == 0)
    def _():
        column_ref[...] = column_of(scale)
        own = face_ref[...] * widen(column_ref[outer:, :], 4 * face) * scale
        other = other_ref[...]
        s = own[:, outer:] + other[:, outer:]
        s = 0.5 * (s + s.T)
        diagonal = jnp.sum(s * eye(face), axis=0, keepdims=True)
        inverse_root = lax.rsqrt(diagonal)
        root_column = column_of(inverse_root)
        s_ref[...] = s * inverse_root * widen(root_column, face)
        invert(s_ref, x_ref, r_ref)
        x = split(x_ref[...])

        def solve(right, at):
            width = right.shape[1]
            weights = widen(root_column, width)
            solved = dot_split(x, split(right * weights)) * weights
            high, low = split(solved)
            high_ref[:, at : at + width] = high
            low_ref[:, at : at + width] = low
            return solved

        solve(own[:, :outer], 0)
        solve(other[:, :outer], outer)
        interface_ref[...] = -solve(product_ref[...], 2 * outer)
        high, low = split(values_ref[...])
        value_high[...] = high
        value_low[...] = low

    block = rows_ref.shape[0]
    column = column_ref[pl.ds(pl.multiple_of(step * block, block), block), :]
    rows = rows_ref[...] * widen(column, 4 * face) * scale
    across = split(rows[:, outer:])

    def through(at, width):
        cut = slice(at, at + width)
        return dot_split(across, (high_ref[:, cut], low_ref[:, cut]))

    merged_ref[:, :outer] = rows[:, :outer] - through(0, outer)
    merged_ref[:, outer:] = -through(outer, outer)
    local = dot_split(split(rows[:, :outer]), (value_high[...], value_low[...]))
    flux_ref[...] = local - through(2 * outer, flux_ref.shape[1])


def pair_solve(operator, values, scale, other_rows, product):
    nodes = operator.shape[1]
    face = nodes // 4
    outer = 3 * face
    count = values.shape[1]
    width = 2 * outer + count
    whole = lambda shape: pl.BlockSpec(shape, lambda i: (0, 0))
    rows = lambda width: pl.BlockSpec((face, width), lambda i: (i, 0))
    return pl.pallas_call(
        solve_kernel,
        grid=(3,),
        in_specs=[
            rows(nodes),
            pl.BlockSpec((face, nodes), lambda i: (3, 0)),
            whole(values.shape),
            whole(scale.shape),
            whole(other_rows.shape),
            whole(product.shape),
        ],
        out_specs=[rows(2 * outer), whole((face, count)), rows(count)],
        out_shape=[
            jax.ShapeDtypeStruct((outer, 2 * outer), F32),
            jax.ShapeDtypeStruct((face, count), F32),
            jax.ShapeDtypeStruct((outer, count), F32),
        ],
        scratch_shapes=[
            pltpu.VMEM((face, width), jnp.bfloat16),
            pltpu.VMEM((face, width), jnp.bfloat16),
            pltpu.VMEM((outer, count), jnp.bfloat16),
            pltpu.VMEM((outer, count), jnp.bfloat16),
            pltpu.VMEM((face, face), F32),
            pltpu.VMEM((face, face), F32),
            pltpu.VMEM((face, face), F32),
            pltpu.VMEM((nodes, 128), F32),
        ],
        compiler_params=pltpu.CompilerParams(vmem_limit_bytes=44 * 2**20),
        name="pair_solve",
    )(operator, operator, values, scale, other_rows, product)


def per_device(
    base_operator, exterior_values, wire_label, wire_material, permittivity, morton_slot
):
    highest = lax.Precision.HIGHEST
    boxes = lax.axis_size("box")
    face = base_operator.shape[1] // 4
    outer = 3 * face
    levels = permittivity.shape[0]
    wires = wire_material.shape[0]
    level_match = wire_material[:, None] == jnp.arange(levels, dtype=jnp.int32)[None, :]
    wire_eps = jnp.sum(jnp.where(level_match, permittivity[None, :], 0.0), axis=1)
    wire_match = wire_label[0][:, None] == jnp.arange(wires, dtype=jnp.int32)[None, :]
    node_scale = jnp.sqrt(jnp.sum(jnp.where(wire_match, wire_eps[None, :], 0.0), axis=1))
    rows = base_operator[outer:, :] * node_scale[outer:, None] * node_scale[None, :]
    positions = jnp.arange(boxes, dtype=jnp.int32)
    slot_match = morton_slot[None, :] == positions[:, None]
    inverse = jnp.sum(jnp.where(slot_match, positions[None, :], 0), axis=1)
    partner = jnp.take(inverse, jnp.bitwise_xor(morton_slot, 1), axis=0)
    product = jnp.dot(rows[:, :outer], exterior_values, precision=highest)
    pieces = lax.all_to_all(
        flatten_rows((rows, product), boxes), "box", split_axis=0, concat_axis=0, tiled=True
    )
    moved = tuple((jnp.take(piece, partner, axis=0) for piece in pieces))
    back = lax.all_to_all(moved, "box", split_axis=0, concat_axis=0, tiled=True)
    other_rows = back[0].reshape(rows.shape)
    other_product = back[1].reshape(product.shape)
    return tuple(
        pair_solve(
            base_operator, exterior_values, node_scale[None, :], other_rows,
            product + other_product,
        )
    )


def solution(mesh):
    return jax.shard_map(
        per_device,
        mesh=mesh,
        in_specs=(P("box", None), P("box", None), P("box", None), P(), P("mc"), P()),
        out_specs=(P(("mc", "box"), None), P(("mc", "box"), None), P(("mc", "box"), None)),
        check_vma=False,
    )
```

```python
import functools

import jax
import jax.numpy as jnp
from jax import lax
from jax.experimental import pallas as pl
from jax.experimental.pallas import tpu as pltpu
from jax.sharding import PartitionSpec as P

F32 = jnp.float32
HIGHEST = lax.Precision.HIGHEST


def split(x):
    high = x.astype(jnp.bfloat16)
    low = (x - high.astype(F32)).astype(jnp.bfloat16)
    return high, low


def dot_split(a, b):
    (ah, al), (bh, bl) = a, b
    dot = functools.partial(jnp.dot, preferred_element_type=F32)
    return dot(ah, bh) + (dot(ah, bl) + dot(al, bh))


def dot3(a, b):
    return dot_split(split(a), split(b))


def column_of(row):
    return jnp.broadcast_to(row, (128, row.shape[1])).T


def widen(column, width):
    return jnp.concatenate([column] * (width // 128), axis=1)


def norm(x):
    return jnp.sqrt(jnp.sum(x * x))


def eye(n):
    row = lax.broadcasted_iota(jnp.int32, (n, n), 0)
    col = lax.broadcasted_iota(jnp.int32, (n, n), 1)
    return jnp.where(row == col, 1.0, 0.0).astype(F32)


def direct_inverse(s_ref, x_ref):
    n = s_ref.shape[0]
    x_ref[...] = s_ref[...]
    row_id = lax.broadcasted_iota(jnp.int32, (n, n), 0)
    col_id = lax.broadcasted_iota(jnp.int32, (n, n), 1)

    def step(k, carry):
        x = x_ref[...]
        on_row = row_id == k
        on_col = col_id == k
        row = jnp.sum(jnp.where(on_row, x, 0.0), axis=0, keepdims=True)
        col = jnp.sum(jnp.where(on_col, x, 0.0), axis=1, keepdims=True)
        pivot = jnp.sum(jnp.where(on_row & on_col, x, 0.0))
        scaled = row / pivot
        rest = x - col * scaled
        x = jnp.where(on_row, scaled, jnp.where(on_col, -col / pivot, rest))
        x_ref[...] = jnp.where(on_row & on_col, 1.0 / pivot, x)
        return carry

    lax.fori_loop(0, n, step, 0)


def invert(s_ref, x_ref, r_ref):
    s = s_ref[...]
    n = s.shape[0]
    unit = eye(n)
    alpha = n / jnp.sum(s * s)

    def begin(alpha):
        first = unit - alpha * s
        x_ref[...] = alpha * (unit + first)
        residual = dot3(first, first)
        r_ref[...] = residual
        return norm(residual)

    size = begin(alpha)

    def safe_start(_):
        return begin(1.0 / jnp.max(jnp.sum(jnp.abs(s), axis=0, keepdims=True)))

    size = lax.cond(size < 0.9, lambda size: size, safe_start, size)
    s_parts = split(s)

    def going(state):
        size, count = state
        return (size > 1e-2) & (count < 40)

    def improve(state):
        size, count = state
        x = x_ref[...]
        x = x + dot3(x, r_ref[...])
        x_ref[...] = x
        residual = unit - dot_split(s_parts, split(x))
        r_ref[...] = residual
        return norm(residual), count + 1

    size, _ = lax.while_loop(going, improve, (size, jnp.int32(0)))
    x = x_ref[...]
    x = x + dot3(x, r_ref[...])
    residual = unit - jnp.dot(s, x, precision=HIGHEST, preferred_element_type=F32)
    x_ref[...] = x + dot3(x, residual)
    converged = (size < 1e-2) & (norm(residual) < 1e-3)

    @pl.when(jnp.logical_not(converged))
    def _():
        direct_inverse(s_ref, x_ref)


def solve_kernel(
    rows_ref, face_ref, values_ref, scale_ref, other_ref, product_ref,
    merged_ref, interface_ref, flux_ref,
    high_ref, low_ref, value_high, value_low, s_ref, x_ref, r_ref, column_ref,
):
    face = face_ref.shape[0]
    outer = 3 * face
    step = pl.program_id(0)
    scale = scale_ref[...]

    @pl.when(step == 0)
    def _():
        column_ref[...] = column_of(scale)
        own = face_ref[...] * widen(column_ref[outer:, :], 4 * face) * scale
        other = other_ref[...]
        s = own[:, outer:] + other[:, outer:]
        s = 0.5 * (s + s.T)
        diagonal = jnp.sum(s * eye(face), axis=0, keepdims=True)
        inverse_root = lax.rsqrt(diagonal)
        root_column = column_of(inverse_root)
        s_ref[...] = s * inverse_root * widen(root_column, face)
        invert(s_ref, x_ref, r_ref)
        x = split(x_ref[...])

        def solve(right, at):
            width = right.shape[1]
            weights = widen(root_column, width)
            solved = dot_split(x, split(right * weights)) * weights
            high, low = split(solved)
            high_ref[:, at : at + width] = high
            low_ref[:, at : at + width] = low
            return solved

        solve(own[:, :outer], 0)
        solve(other[:, :outer], outer)
        interface_ref[...] = -solve(product_ref[...], 2 * outer)
        high, low = split(values_ref[...])
        value_high[...] = high
        value_low[...] = low

    block = rows_ref.shape[0]
    column = column_ref[pl.ds(pl.multiple_of(step * block, block), block), :]
    rows = rows_ref[...] * widen(column, 4 * face) * scale
    across = split(rows[:, outer:])

    def through(at, width):
        cut = slice(at, at + width)
        return dot_split(across, (high_ref[:, cut], low_ref[:, cut]))

    merged_ref[:, :outer] = rows[:, :outer] - through(0, outer)
    merged_ref[:, outer:] = -through(outer, outer)
    local = dot_split(split(rows[:, :outer]), (value_high[...], value_low[...]))
    flux_ref[...] = local - through(2 * outer, flux_ref.shape[1])


def pair_solve(operator, values, scale, other_rows, product):
    nodes = operator.shape[1]
    face = nodes // 4
    outer = 3 * face
    count = values.shape[1]
    width = 2 * outer + count
    whole = lambda shape: pl.BlockSpec(shape, lambda i: (0, 0))
    rows = lambda width: pl.BlockSpec((face, width), lambda i: (i, 0))
    return pl.pallas_call(
        solve_kernel,
        grid=(3,),
        in_specs=[
            rows(nodes),
            pl.BlockSpec((face, nodes), lambda i: (3, 0)),
            whole(values.shape),
            whole(scale.shape),
            whole(other_rows.shape),
            whole(product.shape),
        ],
        out_specs=[rows(2 * outer), whole((face, count)), rows(count)],
        out_shape=[
            jax.ShapeDtypeStruct((outer, 2 * outer), F32),
            jax.ShapeDtypeStruct((face, count), F32),
            jax.ShapeDtypeStruct((outer, count), F32),
        ],
        scratch_shapes=[
            pltpu.VMEM((face, width), jnp.bfloat16),
            pltpu.VMEM((face, width), jnp.bfloat16),
            pltpu.VMEM((outer, count), jnp.bfloat16),
            pltpu.VMEM((outer, count), jnp.bfloat16),
            pltpu.VMEM((face, face), F32),
            pltpu.VMEM((face, face), F32),
            pltpu.VMEM((face, face), F32),
            pltpu.VMEM((nodes, 128), F32),
        ],
        compiler_params=pltpu.CompilerParams(vmem_limit_bytes=44 * 2**20),
        name="pair_solve",
    )(operator, operator, values, scale, other_rows, product)


def exchange_kernel(
    boxes, samples,
    face_ref, values_ref, label_ref, material_ref, permittivity_ref, slot_ref,
    other_ref, total_ref, scale_ref,
    message, gathered, staged, final, partner,
    send_first, receive_first, send_second, receive_second, send_third, receive_third,
):
    me = lax.axis_index("box")
    sample = lax.axis_index("mc")
    face, nodes = face_ref.shape
    outer = 3 * face
    share = face // samples
    across = max(1, boxes * 8 // share)
    width = nodes // across
    height = share * across // boxes
    tiles = width // 128
    part = height * tiles
    strip = face // boxes
    shift = lambda k: lax.rem(me + k + boxes, boxes)
    target = lambda box: {"box": box, "mc": sample}

    barrier = pltpu.get_barrier_semaphore()

    def greet(k, carry):
        pl.semaphore_signal(
            barrier, inc=1, device_id=target(shift(k)), device_id_type=pl.DeviceIdType.MESH
        )
        return carry

    lax.fori_loop(1, boxes, greet, 0)
    twins = [lax.rem(sample + t, samples) for t in range(1, samples)]
    for twin in twins:
        pl.semaphore_signal(
            barrier, inc=1, device_id={"box": me, "mc": twin},
            device_id_type=pl.DeviceIdType.MESH,
        )

    def place(j):
        row = (j // across) * height
        column = lax.rem(j, across) * width
        return row, column

    def fill(j, carry):
        row, column = place(j)
        for t in range(tiles):
            message[j, t * height : (t + 1) * height, :] = face_ref[
                pl.ds(pl.multiple_of(sample * share + row, 8), height),
                pl.ds(pl.multiple_of(column + 128 * t, 128), 128),
            ]
        return carry

    lax.fori_loop(0, boxes, fill, 0)

    label = label_ref[...]
    level = jnp.zeros_like(label)
    for w in range(material_ref.shape[0]):
        level = jnp.where(label == w, material_ref[w], level)
    eps = jnp.zeros(label.shape, F32)
    for l in range(permittivity_ref.shape[0]):
        eps = jnp.where(level == l, permittivity_ref[l], eps)
    root = jnp.sqrt(eps)
    as_row = lambda x: jnp.concatenate([x[t : t + 1, :] for t in range(x.shape[0])], axis=1)
    scale = as_row(root)
    scale_ref[...] = scale
    column = column_of(scale[:, outer:])
    own = face_ref[:, :outer] * widen(column, outer) * scale[:, :outer]
    product = dot3(own, values_ref[...])
    total_ref[...] = product
    for j in range(boxes):
        message[j, part : part + strip, :] = product[j * strip : (j + 1) * strip, :]
    tail = message.shape[1] - root.shape[0]
    message[:, tail:, :] = jnp.broadcast_to(root[None], (boxes,) + root.shape)

    pl.semaphore_wait(barrier, boxes - 1 + samples - 1)

    def first(k, carry):
        box = shift(k)
        pltpu.make_async_remote_copy(
            src_ref=message.at[box], dst_ref=gathered.at[me],
            send_sem=send_first, recv_sem=receive_first,
            device_id=target(box), device_id_type=pl.DeviceIdType.MESH,
        ).start()
        return carry

    lax.fori_loop(1, boxes, first, 0)
    gathered[me] = message[me]

    def find(p, carry):
        wanted = slot_ref[p] ^ 1
        partner[p] = lax.fori_loop(
            0, boxes, lambda i, at: jnp.where(slot_ref[i] == wanted, i, at), jnp.int32(0)
        )
        return carry

    lax.fori_loop(0, boxes, find, 0)

    def drain(buffer, semaphore):
        pltpu.make_async_copy(buffer, buffer, semaphore).wait()

    drain(gathered.at[pl.ds(0, boxes - 1)], receive_first)

    kept = staged.shape[1]

    def stage(p, carry):
        staged[p] = gathered[partner[p], 0:kept, :]
        return carry

    lax.fori_loop(0, boxes, stage, 0)

    def second(k, carry):
        box = shift(k)
        pltpu.make_async_remote_copy(
            src_ref=staged.at[box], dst_ref=final.at[sample, me],
            send_sem=send_second, recv_sem=receive_second.at[k],
            device_id=target(box), device_id_type=pl.DeviceIdType.MESH,
        ).start()
        return carry

    lax.fori_loop(1, boxes, second, 0)
    final[sample, me] = staged[me]

    def forward(source):
        for t, twin in enumerate(twins):
            block = final.at[sample, source, pl.ds(0, part)]
            pltpu.make_async_remote_copy(
                src_ref=block, dst_ref=block,
                send_sem=send_third.at[t], recv_sem=receive_third.at[t],
                device_id={"box": me, "mc": twin}, device_id_type=pl.DeviceIdType.MESH,
            ).start()

    forward(me)

    def third(k, carry):
        source = shift(-k)
        drain(final.at[sample, source], receive_second.at[k])
        forward(source)
        return carry

    lax.fori_loop(1, boxes, third, 0)

    partner_scale = as_row(gathered[partner[me], tail:, :])
    partner_column = column_of(partner_scale[:, outer:])

    def collect(group):
        def body(j, carry):
            row, column = place(j)
            for t in range(tiles):
                other_ref[
                    pl.ds(pl.multiple_of(group * share + row, 8), height),
                    pl.ds(pl.multiple_of(column + 128 * t, 128), 128),
                ] = final[group, j, t * height : (t + 1) * height, :]
            return carry

        lax.fori_loop(0, boxes, body, 0)

    collect(sample)
    for j in range(boxes):
        total_ref[j * strip : (j + 1) * strip, :] += final[sample, j, part : part + strip, :]
    for t, twin in enumerate(twins):
        origin = lax.rem(sample + samples - (t + 1), samples)
        drain(final.at[origin, :, pl.ds(0, part)], receive_third.at[t])
        collect(origin)
    other_ref[...] = other_ref[...] * widen(partner_column, nodes) * partner_scale

    drain(message.at[pl.ds(0, boxes - 1)], send_first)
    drain(staged.at[pl.ds(0, boxes - 1)], send_second)
    for t in range(samples - 1):
        drain(final.at[sample, :, pl.ds(0, part)], send_third.at[t])


def exchange(operator, values, label, material, permittivity, slot):
    boxes = lax.axis_size("box")
    samples = lax.axis_size("mc")
    nodes = operator.shape[1]
    face = nodes // 4
    count = values.shape[1]
    label = label.reshape(nodes // 128, 128)
    part = face // samples * nodes // boxes // 128
    strip = -(-face // boxes // 8) * 8
    kept = part + strip
    whole = lambda shape: pl.BlockSpec(shape, lambda i: (0, 0))
    scalars = pl.BlockSpec(memory_space=pltpu.SMEM)
    return pl.pallas_call(
        functools.partial(exchange_kernel, boxes, samples),
        grid=(1,),
        in_specs=[
            pl.BlockSpec((face, nodes), lambda i: (3, 0)),
            whole(values.shape),
            whole(label.shape),
            scalars,
            scalars,
            scalars,
        ],
        out_specs=[whole((face, nodes)), whole((face, count)), whole((1, nodes))],
        out_shape=[
            jax.ShapeDtypeStruct((face, nodes), F32),
            jax.ShapeDtypeStruct((face, count), F32),
            jax.ShapeDtypeStruct((1, nodes), F32),
        ],
        scratch_shapes=[
            pltpu.VMEM((boxes, kept + nodes // 128, 128), F32),
            pltpu.VMEM((boxes, kept + nodes // 128, 128), F32),
            pltpu.VMEM((boxes, kept, 128), F32),
            pltpu.VMEM((samples, boxes, kept, 128), F32),
            pltpu.SMEM((boxes,), jnp.int32),
            pltpu.SemaphoreType.DMA,
            pltpu.SemaphoreType.DMA,
            pltpu.SemaphoreType.DMA,
            pltpu.SemaphoreType.DMA((boxes,)),
            pltpu.SemaphoreType.DMA((max(1, samples - 1),)),
            pltpu.SemaphoreType.DMA((max(1, samples - 1),)),
        ],
        compiler_params=pltpu.CompilerParams(
            collective_id=0, has_side_effects=True, vmem_limit_bytes=32 * 2**20
        ),
        name="exchange",
    )(operator, values, label, material, permittivity, slot)


def per_device(
    base_operator, exterior_values, wire_label, wire_material, permittivity, morton_slot
):
    other_rows, product, scale = exchange(
        base_operator, exterior_values, wire_label, wire_material, permittivity, morton_slot
    )
    return tuple(pair_solve(base_operator, exterior_values, scale, other_rows, product))


def solution(mesh):
    return jax.shard_map(
        per_device,
        mesh=mesh,
        in_specs=(P("box", None), P("box", None), P("box", None), P(), P("mc"), P()),
        out_specs=(P(("mc", "box"), None), P(("mc", "box"), None), P(("mc", "box"), None)),
        check_vma=False,
    )
```

```python
import functools

import jax
import jax.numpy as jnp
from jax import lax
from jax.experimental import pallas as pl
from jax.experimental.pallas import tpu as pltpu
from jax.sharding import PartitionSpec as P

F32 = jnp.float32
HIGHEST = lax.Precision.HIGHEST


def split(x):
    high = x.astype(jnp.bfloat16)
    low = (x - high.astype(F32)).astype(jnp.bfloat16)
    return high, low


def dot_split(a, b):
    (ah, al), (bh, bl) = a, b
    dot = functools.partial(jnp.dot, preferred_element_type=F32)
    return dot(ah, bh) + (dot(ah, bl) + dot(al, bh))


def dot3(a, b):
    return dot_split(split(a), split(b))


def column_of(row):
    return jnp.broadcast_to(row, (128, row.shape[1])).T


def widen(column, width):
    return jnp.concatenate([column] * (width // 128), axis=1)


def norm(x):
    return jnp.sqrt(jnp.sum(x * x))


def eye(n):
    row = lax.broadcasted_iota(jnp.int32, (n, n), 0)
    col = lax.broadcasted_iota(jnp.int32, (n, n), 1)
    return jnp.where(row == col, 1.0, 0.0).astype(F32)


def direct_inverse(s_ref, x_ref):
    n = s_ref.shape[0]
    x_ref[...] = s_ref[...]
    row_id = lax.broadcasted_iota(jnp.int32, (n, n), 0)
    col_id = lax.broadcasted_iota(jnp.int32, (n, n), 1)

    def step(k, carry):
        x = x_ref[...]
        on_row = row_id == k
        on_col = col_id == k
        row = jnp.sum(jnp.where(on_row, x, 0.0), axis=0, keepdims=True)
        col = jnp.sum(jnp.where(on_col, x, 0.0), axis=1, keepdims=True)
        pivot = jnp.sum(jnp.where(on_row & on_col, x, 0.0))
        scaled = row / pivot
        rest = x - col * scaled
        x = jnp.where(on_row, scaled, jnp.where(on_col, -col / pivot, rest))
        x_ref[...] = jnp.where(on_row & on_col, 1.0 / pivot, x)
        return carry

    lax.fori_loop(0, n, step, 0)


def invert(s_ref, x_ref, r_ref):
    s = s_ref[...]
    n = s.shape[0]
    unit = eye(n)
    alpha = n / jnp.sum(s * s)

    def begin(alpha):
        first = unit - alpha * s
        x_ref[...] = alpha * (unit + first)
        residual = dot3(first, first)
        r_ref[...] = residual
        return norm(residual)

    size = begin(alpha)

    def safe_start(_):
        return begin(1.0 / jnp.max(jnp.sum(jnp.abs(s), axis=0, keepdims=True)))

    size = lax.cond(size < 0.9, lambda size: size, safe_start, size)
    s_parts = split(s)

    def going(state):
        size, count = state
        return (size > 1e-2) & (count < 40)

    def improve(state):
        size, count = state
        x = x_ref[...]
        x = x + dot3(x, r_ref[...])
        x_ref[...] = x
        residual = unit - dot_split(s_parts, split(x))
        r_ref[...] = residual
        return norm(residual), count + 1

    size, _ = lax.while_loop(going, improve, (size, jnp.int32(0)))
    x = x_ref[...]
    x = x + dot3(x, r_ref[...])
    residual = unit - jnp.dot(s, x, precision=HIGHEST, preferred_element_type=F32)
    x_ref[...] = x + dot3(x, residual)
    converged = (size < 1e-2) & (norm(residual) < 1e-3)

    @pl.when(jnp.logical_not(converged))
    def _():
        direct_inverse(s_ref, x_ref)


def solve_kernel(
    rows_ref, face_ref, values_ref, scale_ref, schur_ref, other_ref, product_ref,
    merged_ref, interface_ref, flux_ref,
    high_ref, low_ref, value_high, value_low, s_ref, x_ref, r_ref, column_ref,
):
    face = face_ref.shape[0]
    outer = 3 * face
    step = pl.program_id(0)
    scale = scale_ref[...]

    @pl.when(step == 0)
    def _():
        column_ref[...] = column_of(scale)
        own = face_ref[...] * widen(column_ref[outer:, :], 4 * face) * scale
        s = schur_ref[...]
        diagonal = jnp.sum(s * eye(face), axis=0, keepdims=True)
        inverse_root = lax.rsqrt(diagonal)
        root_column = column_of(inverse_root)
        s_ref[...] = s * inverse_root * widen(root_column, face)
        invert(s_ref, x_ref, r_ref)
        x = split(x_ref[...])

        def solve(right, at):
            width = right.shape[1]
            weights = widen(root_column, width)
            solved = dot_split(x, split(right * weights)) * weights
            high, low = split(solved)
            high_ref[:, at : at + width] = high
            low_ref[:, at : at + width] = low
            return solved

        solve(own[:, :outer], 0)
        solve(other_ref[...], outer)
        interface_ref[...] = -solve(product_ref[...], 2 * outer)
        high, low = split(values_ref[...])
        value_high[...] = high
        value_low[...] = low

    block = rows_ref.shape[0]
    column = column_ref[pl.ds(pl.multiple_of(step * block, block), block), :]
    rows = rows_ref[...] * widen(column, 4 * face) * scale
    across = split(rows[:, outer:])

    def through(at, width):
        cut = slice(at, at + width)
        return dot_split(across, (high_ref[:, cut], low_ref[:, cut]))

    merged_ref[:, :outer] = rows[:, :outer] - through(0, outer)
    merged_ref[:, outer:] = -through(outer, outer)
    local = dot_split(split(rows[:, :outer]), (value_high[...], value_low[...]))
    flux_ref[...] = local - through(2 * outer, flux_ref.shape[1])


def pair_solve(operator, values, scale, schur, other_rows, product):
    nodes = operator.shape[1]
    face = nodes // 4
    outer = 3 * face
    count = values.shape[1]
    width = 2 * outer + count
    whole = lambda shape: pl.BlockSpec(shape, lambda i: (0, 0))
    rows = lambda width: pl.BlockSpec((face, width), lambda i: (i, 0))
    return pl.pallas_call(
        solve_kernel,
        grid=(3,),
        in_specs=[
            rows(nodes),
            pl.BlockSpec((face, nodes), lambda i: (3, 0)),
            whole(values.shape),
            whole(scale.shape),
            whole(schur.shape),
            whole(other_rows.shape),
            whole(product.shape),
        ],
        out_specs=[rows(2 * outer), whole((face, count)), rows(count)],
        out_shape=[
            jax.ShapeDtypeStruct((outer, 2 * outer), F32),
            jax.ShapeDtypeStruct((face, count), F32),
            jax.ShapeDtypeStruct((outer, count), F32),
        ],
        scratch_shapes=[
            pltpu.VMEM((face, width), jnp.bfloat16),
            pltpu.VMEM((face, width), jnp.bfloat16),
            pltpu.VMEM((outer, count), jnp.bfloat16),
            pltpu.VMEM((outer, count), jnp.bfloat16),
            pltpu.VMEM((face, face), F32),
            pltpu.VMEM((face, face), F32),
            pltpu.VMEM((face, face), F32),
            pltpu.VMEM((nodes, 128), F32),
        ],
        compiler_params=pltpu.CompilerParams(vmem_limit_bytes=60 * 2**20),
        name="pair_solve",
    )(operator, operator, values, scale, schur, other_rows, product)


def group_ends(n, expand):
    row = lax.broadcasted_iota(jnp.int32, (n, n), 0)
    col = lax.broadcasted_iota(jnp.int32, (n, n), 1)
    take = (row < n // 2) & (col // 2 == row) if expand else (col < n // 2) & (row == 2 * col)
    return jnp.where(take, 1.0, 0.0).astype(F32)


def exact_dot(a, b):
    return jnp.dot(a, b, precision=HIGHEST, preferred_element_type=F32)


def as_row(x):
    return jnp.concatenate([x[t : t + 1, :] for t in range(x.shape[0])], axis=1)


def triangle(n):
    row = lax.broadcasted_iota(jnp.int32, (n, n), 0)
    col = lax.broadcasted_iota(jnp.int32, (n, n), 1)
    return row, col


def pack_symmetric(block):
    half = block.shape[0] // 2
    row, col = triangle(half)
    first, last = block[:half, :half], block[half:, half:]
    mixed = jnp.where(row >= col, first, last)
    diagonal = jnp.sum(jnp.where(row == col, last, 0.0), axis=0, keepdims=True)
    return block[half:, :half], mixed, diagonal


def unpack_symmetric(corner, mixed, diagonal):
    half = corner.shape[0]
    row, col = triangle(half)
    turned = mixed.T
    first = jnp.where(row >= col, mixed, turned)
    last = jnp.where(row < col, mixed, jnp.where(row == col, diagonal, turned))
    top = jnp.concatenate([first, corner.T], axis=1)
    return jnp.concatenate([top, jnp.concatenate([corner, last], axis=1)], axis=0)


def plan(boxes, samples, face):
    share = face // samples
    across = max(1, boxes * 8 // share)
    columns = 3 * face if across == 1 else 4 * face
    width = columns // across
    height = share * across // boxes
    return share, across, columns, width, height


def exchange_kernel(
    boxes, samples,
    face_ref, values_ref, label_ref, material_ref, permittivity_ref, slot_ref,
    other_ref, schur_ref, total_ref, scale_ref,
    small, small_in, small_staged, small_final, large_in, large_staged, raw, partner,
    send_small, receive_small, send_large, receive_large,
    send_small_2, receive_small_2, send_large_2, receive_large_2,
    send_twin_small, receive_twin_small, send_twin, receive_twin,
):
    me = lax.axis_index("box")
    sample = lax.axis_index("mc")
    face, nodes = face_ref.shape
    outer = 3 * face
    half = face // 2
    share, across, columns, width, height = plan(boxes, samples, face)
    strip = face // boxes
    corner_strip = share // boxes
    at_strip = -(-corner_strip // 8) * 8
    kept = small_staged.shape[1]
    shift = lambda k: lax.rem(me + k + boxes, boxes)
    target = lambda box: {"box": box, "mc": sample}
    MESH = pl.DeviceIdType.MESH

    barrier = pltpu.get_barrier_semaphore()

    def greet(k, carry):
        pl.semaphore_signal(barrier, inc=1, device_id=target(shift(k)), device_id_type=MESH)
        return carry

    lax.fori_loop(1, boxes, greet, 0)
    twins = [lax.rem(sample + t, samples) for t in range(1, samples)]
    for twin in twins:
        pl.semaphore_signal(
            barrier, inc=1, device_id={"box": me, "mc": twin}, device_id_type=MESH
        )

    def offset(i):
        step = (i + 1) // 2
        return boxes // 2 + jnp.where(lax.rem(i, 2) == 0, step, -step)

    def piece(ref, group, j):
        row = group * share + (j // across) * height
        column = lax.rem(j, across) * width
        return ref.at[
            pl.ds(pl.multiple_of(row, 8), height),
            pl.ds(pl.multiple_of(column, 128), width),
        ]

    label = label_ref[...]
    level = jnp.zeros_like(label)
    for w in range(material_ref.shape[0]):
        level = jnp.where(label == w, material_ref[w], level)
    eps = jnp.zeros(label.shape, F32)
    for l in range(permittivity_ref.shape[0]):
        eps = jnp.where(level == l, permittivity_ref[l], eps)
    root = jnp.sqrt(eps)
    scale = as_row(root)
    scale_ref[...] = scale
    column = column_of(scale[:, outer:])
    own = face_ref[:, :outer] * widen(column, outer) * scale[:, :outer]
    product = dot3(own, values_ref[...])
    total_ref[...] = product

    square = face_ref[:, outer:]
    square = 0.5 * (square + square.T)
    corner, mixed, diagonal = pack_symmetric(square)
    mid = root.shape[1] // 2
    row_id = lax.broadcasted_iota(jnp.int32, root.shape, 0)
    lane_id = lax.broadcasted_iota(jnp.int32, root.shape, 1)
    turned = jnp.concatenate([diagonal[:, mid:], diagonal[:, :mid]], axis=1)
    extra = exact_dot(root, group_ends(2 * mid, False))
    extra = jnp.where((lane_id >= mid) & (row_id == 0), turned, extra)
    extra = jnp.where((lane_id >= mid) & (row_id == 1), diagonal, extra)
    packed = jnp.concatenate([corner, mixed], axis=0)
    mine = packed[:share]
    for group in range(1, samples):
        mine = jnp.where(sample == group, packed[group * share : (group + 1) * share], mine)
    for j in range(boxes):
        small[j, :corner_strip, :] = mine[j * corner_strip : (j + 1) * corner_strip, :]
        small[j, at_strip : at_strip + strip, :] = product[j * strip : (j + 1) * strip, :]
    small[:, kept:, :] = jnp.broadcast_to(extra[None], (boxes,) + extra.shape)
    schur_ref[...] = square * widen(column, face) * scale[:, outer:]

    pl.semaphore_wait(barrier, boxes - 1 + samples - 1)

    def send_all(source, landing, send, receive):
        def body(i, carry):
            k = offset(i)
            box = shift(k)
            pltpu.make_async_remote_copy(
                src_ref=source(box), dst_ref=landing, send_sem=send, recv_sem=receive(k),
                device_id=target(box), device_id_type=MESH,
            ).start()
            return carry

        lax.fori_loop(0, boxes - 1, body, 0)

    def drain(buffer, semaphore):
        pltpu.make_async_copy(buffer, buffer, semaphore).wait()

    others = pl.ds(0, boxes - 1)
    send_all(lambda b: small.at[b], small_in.at[me], send_small, lambda k: receive_small)
    send_all(
        lambda b: piece(face_ref, sample, b), large_in.at[me], send_large,
        lambda k: receive_large,
    )
    small_in[me] = small[me]
    large_in[me] = piece(face_ref, sample, me)[...]

    def find(p, carry):
        wanted = slot_ref[p] ^ 1
        partner[p] = lax.fori_loop(
            0, boxes, lambda i, at: jnp.where(slot_ref[i] == wanted, i, at), jnp.int32(0)
        )
        return carry

    lax.fori_loop(0, boxes, find, 0)

    drain(small_in.at[others], receive_small)

    def stage_small(p, carry):
        small_staged[p] = small_in[partner[p], 0:kept, :]
        return carry

    lax.fori_loop(0, boxes, stage_small, 0)
    send_all(
        lambda b: small_staged.at[b], small_final.at[sample, me], send_small_2,
        lambda k: receive_small_2.at[k],
    )
    small_final[sample, me] = small_staged[me]

    drain(large_in.at[others], receive_large)

    def stage_large(p, carry):
        large_staged[p] = large_in[partner[p]]
        return carry

    lax.fori_loop(0, boxes, stage_large, 0)
    send_all(
        lambda b: large_staged.at[b], piece(raw, sample, me), send_large_2,
        lambda k: receive_large_2.at[k],
    )
    piece(raw, sample, me)[...] = large_staged[me]

    def forward(block, send, receive):
        for t, twin in enumerate(twins):
            pltpu.make_async_remote_copy(
                src_ref=block, dst_ref=block, send_sem=send.at[t], recv_sem=receive.at[t],
                device_id={"box": me, "mc": twin}, device_id_type=MESH,
            ).start()

    small_part = lambda group, j: small_final.at[group, j, pl.ds(0, at_strip)]
    forward(small_part(sample, me), send_twin_small, receive_twin_small)

    def pass_small(i, carry):
        k = offset(i)
        source = shift(-k)
        drain(small_final.at[sample, source], receive_small_2.at[k])
        forward(small_part(sample, source), send_twin_small, receive_twin_small)
        return carry

    lax.fori_loop(0, boxes - 1, pass_small, 0)
    forward(piece(raw, sample, me), send_twin, receive_twin)

    def pass_large(i, carry):
        k = offset(i)
        source = shift(-k)
        drain(piece(raw, sample, source), receive_large_2.at[k])
        forward(piece(raw, sample, source), send_twin, receive_twin)
        return carry

    lax.fori_loop(0, boxes - 1, pass_large, 0)

    extra = small_in[partner[me], kept:, :]
    other_scale = as_row(exact_dot(extra, group_ends(2 * mid, True)))
    diagonal = jnp.concatenate([extra[0:1, mid:], extra[1:2, mid:]], axis=1)
    other_column = column_of(other_scale[:, outer:])
    for j in range(boxes):
        total_ref[j * strip : (j + 1) * strip, :] += small_final[
            sample, j, at_strip : at_strip + strip, :
        ]
    for t in range(samples - 1):
        origin = lax.rem(sample + samples - (t + 1), samples)
        drain(small_final.at[origin, :, pl.ds(0, at_strip)], receive_twin_small.at[t])
    pieces = [
        small_final[group, j, :corner_strip, :]
        for group in range(samples) for j in range(boxes)
    ]
    packed = jnp.concatenate(pieces, axis=0)
    square = unpack_symmetric(packed[:half], packed[half:], diagonal)
    schur_ref[...] += square * widen(other_column, face) * other_scale[:, outer:]

    rows_of = lambda ref, group: ref.at[pl.ds(pl.multiple_of(group * share, 8), share)]
    for t in range(samples - 1):
        origin = lax.rem(sample + samples - (t + 1), samples)
        drain(rows_of(raw, origin), receive_twin.at[t])
    other_ref[...] = raw[:, :outer] * widen(other_column, outer) * other_scale[:, :outer]

    drain(small.at[others], send_small)
    drain(large_in.at[others], send_large)
    drain(small_staged.at[others], send_small_2)
    drain(large_staged.at[others], send_large_2)
    for t in range(samples - 1):
        drain(small_final.at[sample, :, pl.ds(0, at_strip)], send_twin_small.at[t])
        drain(rows_of(raw, sample), send_twin.at[t])


def exchange(operator, values, label, material, permittivity, slot):
    boxes = lax.axis_size("box")
    samples = lax.axis_size("mc")
    nodes = operator.shape[1]
    face = nodes // 4
    outer = 3 * face
    count = values.shape[1]
    label = label.reshape(nodes // 128, 128)
    share, across, columns, width, height = plan(boxes, samples, face)
    kept = -(-(share // boxes) // 8) * 8 + -(-(face // boxes) // 8) * 8
    whole = lambda shape: pl.BlockSpec(shape, lambda i: (0, 0))
    scalars = pl.BlockSpec(memory_space=pltpu.SMEM)
    dma = pltpu.SemaphoreType.DMA
    shapes = [(face, outer), (face, face), (face, count), (1, nodes)]
    return pl.pallas_call(
        functools.partial(exchange_kernel, boxes, samples),
        grid=(1,),
        in_specs=[
            pl.BlockSpec((face, nodes), lambda i: (3, 0)),
            whole(values.shape),
            whole(label.shape),
            scalars,
            scalars,
            scalars,
        ],
        out_specs=[whole(shape) for shape in shapes],
        out_shape=[jax.ShapeDtypeStruct(shape, F32) for shape in shapes],
        scratch_shapes=[
            pltpu.VMEM((boxes, kept + nodes // 128, 128), F32),
            pltpu.VMEM((boxes, kept + nodes // 128, 128), F32),
            pltpu.VMEM((boxes, kept, 128), F32),
            pltpu.VMEM((samples, boxes, kept, 128), F32),
            pltpu.VMEM((boxes, height, width), F32),
            pltpu.VMEM((boxes, height, width), F32),
            pltpu.VMEM((face, columns), F32),
            pltpu.SMEM((boxes,), jnp.int32),
            dma, dma, dma, dma,
            dma, dma((boxes,)), dma, dma((boxes,)),
            dma((max(1, samples - 1),)), dma((max(1, samples - 1),)),
            dma((max(1, samples - 1),)), dma((max(1, samples - 1),)),
        ],
        compiler_params=pltpu.CompilerParams(
            collective_id=0, has_side_effects=True, vmem_limit_bytes=60 * 2**20
        ),
        name="exchange",
    )(operator, values, label, material, permittivity, slot)


def per_device(
    base_operator, exterior_values, wire_label, wire_material, permittivity, morton_slot
):
    other_rows, schur, product, scale = exchange(
        base_operator, exterior_values, wire_label, wire_material, permittivity, morton_slot
    )
    return tuple(
        pair_solve(base_operator, exterior_values, scale, schur, other_rows, product)
    )


def solution(mesh):
    return jax.shard_map(
        per_device,
        mesh=mesh,
        in_specs=(P("box", None), P("box", None), P("box", None), P(), P("mc"), P()),
        out_specs=(P(("mc", "box"), None), P(("mc", "box"), None), P(("mc", "box"), None)),
        check_vma=False,
    )
```

```python
import functools

import jax
import jax.numpy as jnp
from jax import lax
from jax.experimental import pallas as pl
from jax.experimental.pallas import tpu as pltpu
from jax.sharding import PartitionSpec as P

F32 = jnp.float32
HIGHEST = lax.Precision.HIGHEST


def split(x):
    high = x.astype(jnp.bfloat16)
    low = (x - high.astype(F32)).astype(jnp.bfloat16)
    return high, low


def dot_split(a, b):
    (ah, al), (bh, bl) = a, b
    dot = functools.partial(jnp.dot, preferred_element_type=F32)
    return dot(ah, bh) + (dot(ah, bl) + dot(al, bh))


def dot3(a, b):
    return dot_split(split(a), split(b))


def column_of(row):
    return jnp.broadcast_to(row, (128, row.shape[1])).T


def widen(column, width):
    return jnp.concatenate([column] * (width // 128), axis=1)


def norm(x):
    return jnp.sqrt(jnp.sum(x * x))


def eye(n):
    row = lax.broadcasted_iota(jnp.int32, (n, n), 0)
    col = lax.broadcasted_iota(jnp.int32, (n, n), 1)
    return jnp.where(row == col, 1.0, 0.0).astype(F32)


def direct_inverse(s_ref, x_ref):
    n = s_ref.shape[0]
    x_ref[...] = s_ref[...]
    row_id = lax.broadcasted_iota(jnp.int32, (n, n), 0)
    col_id = lax.broadcasted_iota(jnp.int32, (n, n), 1)

    def step(k, carry):
        x = x_ref[...]
        on_row = row_id == k
        on_col = col_id == k
        row = jnp.sum(jnp.where(on_row, x, 0.0), axis=0, keepdims=True)
        col = jnp.sum(jnp.where(on_col, x, 0.0), axis=1, keepdims=True)
        pivot = jnp.sum(jnp.where(on_row & on_col, x, 0.0))
        scaled = row / pivot
        rest = x - col * scaled
        x = jnp.where(on_row, scaled, jnp.where(on_col, -col / pivot, rest))
        x_ref[...] = jnp.where(on_row & on_col, 1.0 / pivot, x)
        return carry

    lax.fori_loop(0, n, step, 0)


def invert(s_ref, x_ref, r_ref):
    s = s_ref[...]
    n = s.shape[0]
    unit = eye(n)
    alpha = n / jnp.sum(s * s)

    def begin(alpha):
        first = unit - alpha * s
        x_ref[...] = alpha * (unit + first)
        residual = dot3(first, first)
        r_ref[...] = residual
        return norm(residual)

    size = begin(alpha)

    def safe_start(_):
        return begin(1.0 / jnp.max(jnp.sum(jnp.abs(s), axis=0, keepdims=True)))

    size = lax.cond(size < 0.9, lambda size: size, safe_start, size)
    s_parts = split(s)

    def going(state):
        size, count = state
        return (size > 1e-2) & (count < 40)

    def improve(state):
        size, count = state
        x = x_ref[...]
        x = x + dot3(x, r_ref[...])
        x_ref[...] = x
        residual = unit - dot_split(s_parts, split(x))
        r_ref[...] = residual
        return norm(residual), count + 1

    size, _ = lax.while_loop(going, improve, (size, jnp.int32(0)))
    x = x_ref[...]
    x = x + dot3(x, r_ref[...])
    residual = unit - jnp.dot(s, x, precision=HIGHEST, preferred_element_type=F32)
    x_ref[...] = x + dot3(x, residual)
    converged = (size < 1e-2) & (norm(residual) < 1e-3)

    @pl.when(jnp.logical_not(converged))
    def _():
        direct_inverse(s_ref, x_ref)


def fixed_inverse(s):
    n = s.shape[0]
    unit = eye(n)
    alpha = n / jnp.sum(s * s)
    first = unit - alpha * s
    parts = split(s)
    x = alpha * (unit + first)
    residual = dot3(first, first)
    yield None
    x = x + dot3(x, residual)
    yield None
    residual = unit - dot_split(parts, split(x))
    yield None
    x = x + dot3(x, residual)
    yield None
    residual = unit - exact_dot(s, x)
    yield None
    yield x + dot3(x, residual), norm(residual)


def finish_kernel(
    left_ref, through_ref, other_ref, interface_in, flux_in, residual_ref,
    operator_ref, values_ref, scale_ref, schur_ref, product_ref,
    merged_ref, interface_ref, flux_ref,
    other_high, other_low, solved_high, solved_low, rows, s_ref, x_ref, r_ref, column_ref,
    values, schur, product, semaphore,
):
    block = left_ref.shape[0]
    face, outer = other_ref.shape
    step = pl.program_id(0)
    fast = residual_ref[0, 0] < 1e-3

    @pl.when(fast)
    def _():
        @pl.when(step == 0)
        def _():
            high, low = split(other_ref[...])
            other_high[...] = high
            other_low[...] = low
            interface_ref[...] = interface_in[...]

        merged_ref[:, :outer] = left_ref[...]
        through = split(through_ref[...])
        merged_ref[:, outer:] = -dot_split(through, (other_high[...], other_low[...]))
        flux_ref[...] = flux_in[...]

    def fetch(source, target):
        copy = pltpu.make_async_copy(source, target, semaphore)
        copy.start()
        copy.wait()

    @pl.when(jnp.logical_not(fast))
    def _():
        scale = scale_ref[...]

        @pl.when(step == 0)
        def _():
            column_ref[...] = column_of(scale)
            fetch(operator_ref.at[pl.ds(outer, face)], rows)
            fetch(values_ref, values)
            fetch(schur_ref, schur)
            fetch(product_ref, product)
            own = rows[:, :outer] * widen(column_ref[outer:, :], outer) * scale[:, :outer]
            s = schur[...]
            inverse_root = lax.rsqrt(jnp.sum(s * eye(face), axis=0, keepdims=True))
            root_column = column_of(inverse_root)
            s_ref[...] = s * inverse_root * widen(root_column, face)
            invert(s_ref, x_ref, r_ref)
            x = split(x_ref[...])

            def solve(right, at):
                width = right.shape[1]
                weights = widen(root_column, width)
                solved = dot_split(x, split(right * weights)) * weights
                high, low = split(solved)
                solved_high[:, at : at + width] = high
                solved_low[:, at : at + width] = low
                return solved

            solve(own, 0)
            solve(other_ref[...], outer)
            interface_ref[...] = -solve(product[...], 2 * outer)

        at = pl.multiple_of(step * block, block)
        fetch(operator_ref.at[pl.ds(at, block)], rows)
        mine = rows[...] * widen(column_ref[pl.ds(at, block), :], 4 * face) * scale
        across = split(mine[:, outer:])

        def apply(at, width):
            cut = slice(at, at + width)
            return dot_split(across, (solved_high[:, cut], solved_low[:, cut]))

        merged_ref[:, :outer] = mine[:, :outer] - apply(0, outer)
        merged_ref[:, outer:] = -apply(outer, outer)
        local = dot3(mine[:, :outer], values[...])
        flux_ref[...] = local - apply(2 * outer, flux_ref.shape[1])


def finish(left, through, other, interface, flux, residual, operator, values, scale, schur, product):
    outer = left.shape[0]
    face = outer // 3
    nodes = 4 * face
    count = values.shape[1]
    width = 2 * outer + count
    whole = lambda x: pl.BlockSpec(x.shape, lambda i: (0, 0))
    rows = lambda width: pl.BlockSpec((face, width), lambda i: (i, 0))
    anywhere = pl.BlockSpec(memory_space=pl.ANY)
    half = jnp.bfloat16
    return pl.pallas_call(
        finish_kernel,
        grid=(3,),
        in_specs=[
            rows(outer), rows(face), whole(other), whole(interface), rows(count),
            pl.BlockSpec(memory_space=pltpu.SMEM),
            anywhere, anywhere, whole(scale), anywhere, anywhere,
        ],
        out_specs=[rows(2 * outer), whole(interface), rows(count)],
        out_shape=[
            jax.ShapeDtypeStruct((outer, 2 * outer), F32),
            jax.ShapeDtypeStruct((face, count), F32),
            jax.ShapeDtypeStruct((outer, count), F32),
        ],
        scratch_shapes=[
            pltpu.VMEM((face, outer), half),
            pltpu.VMEM((face, outer), half),
            pltpu.VMEM((face, width), half),
            pltpu.VMEM((face, width), half),
            pltpu.VMEM((face, nodes), F32),
            pltpu.VMEM((face, face), F32),
            pltpu.VMEM((face, face), F32),
            pltpu.VMEM((face, face), F32),
            pltpu.VMEM((nodes, 128), F32),
            pltpu.VMEM((outer, count), F32),
            pltpu.VMEM((face, face), F32),
            pltpu.VMEM((face, count), F32),
            pltpu.SemaphoreType.DMA,
        ],
        compiler_params=pltpu.CompilerParams(vmem_limit_bytes=60 * 2**20),
        name="finish",
    )(left, through, other, interface, flux, residual, operator, values, scale, schur, product)


def group_ends(n, expand):
    row = lax.broadcasted_iota(jnp.int32, (n, n), 0)
    col = lax.broadcasted_iota(jnp.int32, (n, n), 1)
    take = (row < n // 2) & (col // 2 == row) if expand else (col < n // 2) & (row == 2 * col)
    return jnp.where(take, 1.0, 0.0).astype(F32)


def exact_dot(a, b):
    return jnp.dot(a, b, precision=HIGHEST, preferred_element_type=F32)


def as_row(x):
    return jnp.concatenate([x[t : t + 1, :] for t in range(x.shape[0])], axis=1)


def triangle(n):
    row = lax.broadcasted_iota(jnp.int32, (n, n), 0)
    col = lax.broadcasted_iota(jnp.int32, (n, n), 1)
    return row, col


def pack_symmetric(block):
    half = block.shape[0] // 2
    row, col = triangle(half)
    first, last = block[:half, :half], block[half:, half:]
    mixed = jnp.where(row >= col, first, last)
    diagonal = jnp.sum(jnp.where(row == col, last, 0.0), axis=0, keepdims=True)
    return block[half:, :half], mixed, diagonal


def unpack_symmetric(corner, mixed, diagonal):
    half = corner.shape[0]
    row, col = triangle(half)
    turned = mixed.T
    first = jnp.where(row >= col, mixed, turned)
    last = jnp.where(row < col, mixed, jnp.where(row == col, diagonal, turned))
    top = jnp.concatenate([first, corner.T], axis=1)
    return jnp.concatenate([top, jnp.concatenate([corner, last], axis=1)], axis=0)


def plan(boxes, samples, face):
    share = face // samples
    across = max(1, boxes * 8 // share)
    columns = 3 * face if across == 1 else 4 * face
    width = columns // across
    height = share * across // boxes
    return share, across, columns, width, height


def exchange_kernel(
    boxes, samples,
    face_ref, values_ref, label_ref, material_ref, permittivity_ref, slot_ref,
    operator_ref,
    left_ref, through_ref, other_ref, interface_ref, flux_ref, residual_ref,
    scale_ref, schur_ref, total_ref,
    rest, load, small, small_in, small_staged, small_final, large_in, large_staged, raw, partner,
    send_small, receive_small, send_large, receive_large,
    send_small_2, receive_small_2, send_large_2, receive_large_2,
    send_twin_small, receive_twin_small, send_twin, receive_twin,
):
    me = lax.axis_index("box")
    sample = lax.axis_index("mc")
    face, nodes = face_ref.shape
    outer = 3 * face
    half = face // 2
    share, across, columns, width, height = plan(boxes, samples, face)
    strip = face // boxes
    corner_strip = share // boxes
    at_strip = -(-corner_strip // 8) * 8
    kept = small_staged.shape[1]
    shift = lambda k: lax.rem(me + k + boxes, boxes)
    target = lambda box: {"box": box, "mc": sample}
    MESH = pl.DeviceIdType.MESH

    rest_copy = pltpu.make_async_copy(operator_ref.at[pl.ds(0, outer)], rest, load)
    rest_copy.start()
    barrier = pltpu.get_barrier_semaphore()

    def greet(k, carry):
        pl.semaphore_signal(barrier, inc=1, device_id=target(shift(k)), device_id_type=MESH)
        return carry

    lax.fori_loop(1, boxes, greet, 0)
    twins = [lax.rem(sample + t, samples) for t in range(1, samples)]
    for twin in twins:
        pl.semaphore_signal(
            barrier, inc=1, device_id={"box": me, "mc": twin}, device_id_type=MESH
        )

    def offset(i):
        step = (i + 1) // 2
        return boxes // 2 + jnp.where(lax.rem(i, 2) == 0, step, -step)

    def piece(ref, group, j):
        row = group * share + (j // across) * height
        column = lax.rem(j, across) * width
        return ref.at[
            pl.ds(pl.multiple_of(row, 8), height),
            pl.ds(pl.multiple_of(column, 128), width),
        ]

    label = label_ref[...]
    level = jnp.zeros_like(label)
    for w in range(material_ref.shape[0]):
        level = jnp.where(label == w, material_ref[w], level)
    eps = jnp.zeros(label.shape, F32)
    for l in range(permittivity_ref.shape[0]):
        eps = jnp.where(level == l, permittivity_ref[l], eps)
    root = jnp.sqrt(eps)
    scale = as_row(root)
    scale_ref[...] = scale
    column = column_of(scale[:, outer:])
    own = face_ref[:, :outer] * widen(column, outer) * scale[:, :outer]
    own_parts = split(own)
    product = dot_split(own_parts, split(values_ref[...]))
    total_ref[...] = product

    square = face_ref[:, outer:]
    square = 0.5 * (square + square.T)
    corner, mixed, diagonal = pack_symmetric(square)
    mid = root.shape[1] // 2
    row_id = lax.broadcasted_iota(jnp.int32, root.shape, 0)
    lane_id = lax.broadcasted_iota(jnp.int32, root.shape, 1)
    turned = jnp.concatenate([diagonal[:, mid:], diagonal[:, :mid]], axis=1)
    extra = exact_dot(root, group_ends(2 * mid, False))
    extra = jnp.where((lane_id >= mid) & (row_id == 0), turned, extra)
    extra = jnp.where((lane_id >= mid) & (row_id == 1), diagonal, extra)
    packed = jnp.concatenate([corner, mixed], axis=0)
    mine = packed[:share]
    for group in range(1, samples):
        mine = jnp.where(sample == group, packed[group * share : (group + 1) * share], mine)
    for j in range(boxes):
        small[j, :corner_strip, :] = mine[j * corner_strip : (j + 1) * corner_strip, :]
        small[j, at_strip : at_strip + strip, :] = product[j * strip : (j + 1) * strip, :]
    small[:, kept:, :] = jnp.broadcast_to(extra[None], (boxes,) + extra.shape)
    schur_ref[...] = square * widen(column, face) * scale[:, outer:]

    pl.semaphore_wait(barrier, boxes - 1 + samples - 1)

    def send_all(source, landing, send, receive):
        def body(i, carry):
            k = offset(i)
            box = shift(k)
            pltpu.make_async_remote_copy(
                src_ref=source(box), dst_ref=landing, send_sem=send, recv_sem=receive(k),
                device_id=target(box), device_id_type=MESH,
            ).start()
            return carry

        lax.fori_loop(0, boxes - 1, body, 0)

    def drain(buffer, semaphore):
        pltpu.make_async_copy(buffer, buffer, semaphore).wait()

    others = pl.ds(0, boxes - 1)
    send_all(lambda b: small.at[b], small_in.at[me], send_small, lambda k: receive_small)
    send_all(
        lambda b: piece(face_ref, sample, b), large_in.at[me], send_large,
        lambda k: receive_large,
    )
    small_in[me] = small[me]
    large_in[me] = piece(face_ref, sample, me)[...]

    def find(p, carry):
        wanted = slot_ref[p] ^ 1
        partner[p] = lax.fori_loop(
            0, boxes, lambda i, at: jnp.where(slot_ref[i] == wanted, i, at), jnp.int32(0)
        )
        return carry

    lax.fori_loop(0, boxes, find, 0)

    rest_copy.wait()
    values_parts = split(values_ref[...])
    for at in range(0, outer, face):
        cut = slice(at, at + face)
        rest[cut, :] = rest[cut, :] * widen(column_of(scale[:, cut]), nodes) * scale
        flux_ref[cut, :] = dot_split(split(rest[cut, :outer]), values_parts)

    drain(small_in.at[others], receive_small)

    def stage_small(p, carry):
        small_staged[p] = small_in[partner[p], 0:kept, :]
        return carry

    lax.fori_loop(0, boxes, stage_small, 0)
    send_all(
        lambda b: small_staged.at[b], small_final.at[sample, me], send_small_2,
        lambda k: receive_small_2.at[k],
    )
    small_final[sample, me] = small_staged[me]

    drain(large_in.at[others], receive_large)

    def stage_large(p, carry):
        large_staged[p] = large_in[partner[p]]
        return carry

    lax.fori_loop(0, boxes, stage_large, 0)
    send_all(
        lambda b: large_staged.at[b], piece(raw, sample, me), send_large_2,
        lambda k: receive_large_2.at[k],
    )
    piece(raw, sample, me)[...] = large_staged[me]

    def forward(block, send, receive):
        for t, twin in enumerate(twins):
            pltpu.make_async_remote_copy(
                src_ref=block, dst_ref=block, send_sem=send.at[t], recv_sem=receive.at[t],
                device_id={"box": me, "mc": twin}, device_id_type=MESH,
            ).start()

    small_part = lambda group, j: small_final.at[group, j, pl.ds(0, at_strip)]
    forward(small_part(sample, me), send_twin_small, receive_twin_small)

    def pass_small(i, carry):
        k = offset(i)
        source = shift(-k)
        drain(small_final.at[sample, source], receive_small_2.at[k])
        forward(small_part(sample, source), send_twin_small, receive_twin_small)
        return carry

    lax.fori_loop(0, boxes - 1, pass_small, 0)
    extra = small_in[partner[me], kept:, :]
    other_scale = as_row(exact_dot(extra, group_ends(2 * mid, True)))
    diagonal = jnp.concatenate([extra[0:1, mid:], extra[1:2, mid:]], axis=1)
    other_column = column_of(other_scale[:, outer:])
    for j in range(boxes):
        total_ref[j * strip : (j + 1) * strip, :] += small_final[
            sample, j, at_strip : at_strip + strip, :
        ]
    for t in range(samples - 1):
        origin = lax.rem(sample + samples - (t + 1), samples)
        drain(small_final.at[origin, :, pl.ds(0, at_strip)], receive_twin_small.at[t])
    pieces = [
        small_final[group, j, :corner_strip, :]
        for group in range(samples) for j in range(boxes)
    ]
    packed = jnp.concatenate(pieces, axis=0)
    square = unpack_symmetric(packed[:half], packed[half:], diagonal)
    schur_ref[...] += square * widen(other_column, face) * other_scale[:, outer:]

    forward(piece(raw, sample, me), send_twin, receive_twin)

    def pass_large(i, carry):
        k = offset(i)
        source = shift(-k)
        drain(piece(raw, sample, source), receive_large_2.at[k])
        forward(piece(raw, sample, source), send_twin, receive_twin)
        return carry

    def work():
        schur = schur_ref[...]
        inverse_root = lax.rsqrt(jnp.sum(schur * eye(face), axis=0, keepdims=True))
        weights = widen(column_of(inverse_root), face) * inverse_root
        for result in fixed_inverse(schur * weights):
            if result is None:
                yield
        x, size = result
        residual_ref[0, 0] = size
        inverse = split(x * weights)
        total = split(total_ref[...])
        interface_ref[...] = -dot_split(inverse, total)
        yield
        for at in range(0, outer, face):
            cut = slice(at, at + face)
            through = dot_split(split(rest[cut, outer:]), inverse)
            through_ref[cut, :] = through
            through = split(through)
            flux_ref[cut, :] -= dot_split(through, total)
            yield
            left_ref[cut, :] = rest[cut, :outer] - dot_split(through, own_parts)
            yield

    parts = 12
    done = 0
    for part, _ in enumerate(work()):
        upto = min(boxes - 1, (part + 1) * (boxes - 1) // parts)
        lax.fori_loop(done, upto, pass_large, 0)
        done = upto
    lax.fori_loop(done, boxes - 1, pass_large, 0)

    rows_of = lambda ref, group: ref.at[pl.ds(pl.multiple_of(group * share, 8), share)]
    for t in range(samples - 1):
        origin = lax.rem(sample + samples - (t + 1), samples)
        drain(rows_of(raw, origin), receive_twin.at[t])
    other_ref[...] = raw[:, :outer] * widen(other_column, outer) * other_scale[:, :outer]

    drain(small.at[others], send_small)
    drain(large_in.at[others], send_large)
    drain(small_staged.at[others], send_small_2)
    drain(large_staged.at[others], send_large_2)
    for t in range(samples - 1):
        drain(small_final.at[sample, :, pl.ds(0, at_strip)], send_twin_small.at[t])
        drain(rows_of(raw, sample), send_twin.at[t])


def exchange(operator, values, label, material, permittivity, slot):
    boxes = lax.axis_size("box")
    samples = lax.axis_size("mc")
    nodes = operator.shape[1]
    face = nodes // 4
    outer = 3 * face
    count = values.shape[1]
    label = label.reshape(nodes // 128, 128)
    share, across, columns, width, height = plan(boxes, samples, face)
    kept = -(-(share // boxes) // 8) * 8 + -(-(face // boxes) // 8) * 8
    whole = lambda shape: pl.BlockSpec(shape, lambda i: (0, 0))
    scalars = pl.BlockSpec(memory_space=pltpu.SMEM)
    dma = pltpu.SemaphoreType.DMA
    shapes = [
        (outer, outer), (outer, face), (face, outer), (face, count), (outer, count), (1, 1),
        (1, nodes), (face, face), (face, count),
    ]
    return pl.pallas_call(
        functools.partial(exchange_kernel, boxes, samples),
        grid=(1,),
        in_specs=[
            pl.BlockSpec((face, nodes), lambda i: (3, 0)),
            whole(values.shape),
            whole(label.shape),
            scalars,
            scalars,
            scalars,
            pl.BlockSpec(memory_space=pl.ANY),
        ],
        out_specs=[scalars if shape == (1, 1) else whole(shape) for shape in shapes],
        out_shape=[jax.ShapeDtypeStruct(shape, F32) for shape in shapes],
        scratch_shapes=[
            pltpu.VMEM((outer, nodes), F32),
            dma,
            pltpu.VMEM((boxes, kept + nodes // 128, 128), F32),
            pltpu.VMEM((boxes, kept + nodes // 128, 128), F32),
            pltpu.VMEM((boxes, kept, 128), F32),
            pltpu.VMEM((samples, boxes, kept, 128), F32),
            pltpu.VMEM((boxes, height, width), F32),
            pltpu.VMEM((boxes, height, width), F32),
            pltpu.VMEM((face, columns), F32),
            pltpu.SMEM((boxes,), jnp.int32),
            dma, dma, dma, dma,
            dma, dma((boxes,)), dma, dma((boxes,)),
            dma((max(1, samples - 1),)), dma((max(1, samples - 1),)),
            dma((max(1, samples - 1),)), dma((max(1, samples - 1),)),
        ],
        compiler_params=pltpu.CompilerParams(
            collective_id=0, has_side_effects=True, vmem_limit_bytes=60 * 2**20
        ),
        name="exchange",
    )(operator, values, label, material, permittivity, slot, operator)


def per_device(
    base_operator, exterior_values, wire_label, wire_material, permittivity, morton_slot
):
    parts = exchange(
        base_operator, exterior_values, wire_label, wire_material, permittivity, morton_slot
    )
    left, through, other, interface, flux, residual, scale, schur, product = parts
    return tuple(
        finish(
            left, through, other, interface, flux, residual,
            base_operator, exterior_values, scale, schur, product,
        )
    )


def solution(mesh):
    return jax.shard_map(
        per_device,
        mesh=mesh,
        in_specs=(P("box", None), P("box", None), P("box", None), P(), P("mc"), P()),
        out_specs=(P(("mc", "box"), None), P(("mc", "box"), None), P(("mc", "box"), None)),
        check_vma=False,
    )
```

```python
import functools

import jax
import jax.numpy as jnp
from jax import lax
from jax.experimental import pallas as pl
from jax.experimental.pallas import tpu as pltpu
from jax.sharding import PartitionSpec as P

F32 = jnp.float32
HIGHEST = lax.Precision.HIGHEST


def split(x):
    high = x.astype(jnp.bfloat16)
    low = (x - high.astype(F32)).astype(jnp.bfloat16)
    return high, low


def dot_split(a, b):
    (ah, al), (bh, bl) = a, b
    dot = functools.partial(jnp.dot, preferred_element_type=F32)
    return dot(ah, bh) + (dot(ah, bl) + dot(al, bh))


def dot3(a, b):
    return dot_split(split(a), split(b))


def column_of(row):
    return jnp.broadcast_to(row, (128, row.shape[1])).T


def widen(column, width):
    return jnp.concatenate([column] * (width // 128), axis=1)


def norm(x):
    return jnp.sqrt(jnp.sum(x * x))


def eye(n):
    row = lax.broadcasted_iota(jnp.int32, (n, n), 0)
    col = lax.broadcasted_iota(jnp.int32, (n, n), 1)
    return jnp.where(row == col, 1.0, 0.0).astype(F32)


def direct_inverse(s_ref, x_ref):
    n = s_ref.shape[0]
    x_ref[...] = s_ref[...]
    row_id = lax.broadcasted_iota(jnp.int32, (n, n), 0)
    col_id = lax.broadcasted_iota(jnp.int32, (n, n), 1)

    def step(k, carry):
        x = x_ref[...]
        on_row = row_id == k
        on_col = col_id == k
        row = jnp.sum(jnp.where(on_row, x, 0.0), axis=0, keepdims=True)
        col = jnp.sum(jnp.where(on_col, x, 0.0), axis=1, keepdims=True)
        pivot = jnp.sum(jnp.where(on_row & on_col, x, 0.0))
        scaled = row / pivot
        rest = x - col * scaled
        x = jnp.where(on_row, scaled, jnp.where(on_col, -col / pivot, rest))
        x_ref[...] = jnp.where(on_row & on_col, 1.0 / pivot, x)
        return carry

    lax.fori_loop(0, n, step, 0)


def invert(s_ref, x_ref, r_ref):
    s = s_ref[...]
    n = s.shape[0]
    unit = eye(n)
    alpha = n / jnp.sum(s * s)

    def begin(alpha):
        first = unit - alpha * s
        x_ref[...] = alpha * (unit + first)
        residual = dot3(first, first)
        r_ref[...] = residual
        return norm(residual)

    size = begin(alpha)

    def safe_start(_):
        return begin(1.0 / jnp.max(jnp.sum(jnp.abs(s), axis=0, keepdims=True)))

    size = lax.cond(size < 0.9, lambda size: size, safe_start, size)
    s_parts = split(s)

    def going(state):
        size, count = state
        return (size > 1e-2) & (count < 40)

    def improve(state):
        size, count = state
        x = x_ref[...]
        x = x + dot3(x, r_ref[...])
        x_ref[...] = x
        residual = unit - dot_split(s_parts, split(x))
        r_ref[...] = residual
        return norm(residual), count + 1

    size, _ = lax.while_loop(going, improve, (size, jnp.int32(0)))
    x = x_ref[...]
    x = x + dot3(x, r_ref[...])
    residual = unit - jnp.dot(s, x, precision=HIGHEST, preferred_element_type=F32)
    x_ref[...] = x + dot3(x, residual)
    converged = (size < 1e-2) & (norm(residual) < 1e-3)

    @pl.when(jnp.logical_not(converged))
    def _():
        direct_inverse(s_ref, x_ref)


def fixed_inverse(s):
    n = s.shape[0]
    unit = eye(n)
    alpha = n / jnp.sum(s * s)
    first = unit - alpha * s
    parts = split(s)
    x = alpha * (unit + first)
    residual = dot3(first, first)
    yield None
    x = x + dot3(x, residual)
    yield None
    residual = unit - dot_split(parts, split(x))
    yield None
    x = x + dot3(x, residual)
    yield None
    residual = unit - exact_dot(s, x)
    yield None
    yield x + dot3(x, residual), norm(residual)


def finish_kernel(
    left_ref, through_ref, other_ref, interface_in, flux_in, residual_ref,
    operator_ref, values_ref, scale_ref, schur_ref, product_ref,
    merged_ref, interface_ref, flux_ref,
    other_high, other_low, solved_high, solved_low, rows, s_ref, x_ref, r_ref, column_ref,
    values, schur, product, semaphore,
):
    block = left_ref.shape[0]
    face, outer = other_ref.shape
    step = pl.program_id(0)
    fast = residual_ref[0, 0] < 1e-3

    @pl.when(fast)
    def _():
        @pl.when(step == 0)
        def _():
            high, low = split(other_ref[...])
            other_high[...] = high
            other_low[...] = low
            interface_ref[...] = interface_in[...]

        merged_ref[:, :outer] = left_ref[...]
        through = split(through_ref[...])
        merged_ref[:, outer:] = -dot_split(through, (other_high[...], other_low[...]))
        flux_ref[...] = flux_in[...]

    def fetch(source, target):
        copy = pltpu.make_async_copy(source, target, semaphore)
        copy.start()
        copy.wait()

    @pl.when(jnp.logical_not(fast))
    def _():
        scale = scale_ref[...]

        @pl.when(step == 0)
        def _():
            column_ref[...] = column_of(scale)
            fetch(operator_ref.at[pl.ds(outer, face)], rows)
            fetch(values_ref, values)
            fetch(schur_ref, schur)
            fetch(product_ref, product)
            own = rows[:, :outer] * widen(column_ref[outer:, :], outer) * scale[:, :outer]
            s = schur[...]
            inverse_root = lax.rsqrt(jnp.sum(s * eye(face), axis=0, keepdims=True))
            root_column = column_of(inverse_root)
            s_ref[...] = s * inverse_root * widen(root_column, face)
            invert(s_ref, x_ref, r_ref)
            x = split(x_ref[...])

            def solve(right, at):
                width = right.shape[1]
                weights = widen(root_column, width)
                solved = dot_split(x, split(right * weights)) * weights
                high, low = split(solved)
                solved_high[:, at : at + width] = high
                solved_low[:, at : at + width] = low
                return solved

            solve(own, 0)
            solve(other_ref[...], outer)
            interface_ref[...] = -solve(product[...], 2 * outer)

        at = pl.multiple_of(step * block, block)
        fetch(operator_ref.at[pl.ds(at, block)], rows)
        mine = rows[...] * widen(column_ref[pl.ds(at, block), :], 4 * face) * scale
        across = split(mine[:, outer:])

        def apply(at, width):
            cut = slice(at, at + width)
            return dot_split(across, (solved_high[:, cut], solved_low[:, cut]))

        merged_ref[:, :outer] = mine[:, :outer] - apply(0, outer)
        merged_ref[:, outer:] = -apply(outer, outer)
        local = dot3(mine[:, :outer], values[...])
        flux_ref[...] = local - apply(2 * outer, flux_ref.shape[1])


def finish(left, through, other, interface, flux, residual, operator, values, scale, schur, product):
    outer = left.shape[0]
    face = outer // 3
    nodes = 4 * face
    count = values.shape[1]
    width = 2 * outer + count
    whole = lambda x: pl.BlockSpec(x.shape, lambda i: (0, 0))
    rows = lambda width: pl.BlockSpec((face, width), lambda i: (i, 0))
    anywhere = pl.BlockSpec(memory_space=pl.ANY)
    half = jnp.bfloat16
    return pl.pallas_call(
        finish_kernel,
        grid=(3,),
        in_specs=[
            rows(outer), rows(face), whole(other), whole(interface), rows(count),
            pl.BlockSpec(memory_space=pltpu.SMEM),
            anywhere, anywhere, whole(scale), anywhere, anywhere,
        ],
        out_specs=[rows(2 * outer), whole(interface), rows(count)],
        out_shape=[
            jax.ShapeDtypeStruct((outer, 2 * outer), F32),
            jax.ShapeDtypeStruct((face, count), F32),
            jax.ShapeDtypeStruct((outer, count), F32),
        ],
        scratch_shapes=[
            pltpu.VMEM((face, outer), half),
            pltpu.VMEM((face, outer), half),
            pltpu.VMEM((face, width), half),
            pltpu.VMEM((face, width), half),
            pltpu.VMEM((face, nodes), F32),
            pltpu.VMEM((face, face), F32),
            pltpu.VMEM((face, face), F32),
            pltpu.VMEM((face, face), F32),
            pltpu.VMEM((nodes, 128), F32),
            pltpu.VMEM((outer, count), F32),
            pltpu.VMEM((face, face), F32),
            pltpu.VMEM((face, count), F32),
            pltpu.SemaphoreType.DMA,
        ],
        compiler_params=pltpu.CompilerParams(vmem_limit_bytes=60 * 2**20),
        name="finish",
    )(left, through, other, interface, flux, residual, operator, values, scale, schur, product)


def group_ends(n, expand):
    row = lax.broadcasted_iota(jnp.int32, (n, n), 0)
    col = lax.broadcasted_iota(jnp.int32, (n, n), 1)
    take = (row < n // 2) & (col // 2 == row) if expand else (col < n // 2) & (row == 2 * col)
    return jnp.where(take, 1.0, 0.0).astype(F32)


def exact_dot(a, b):
    return jnp.dot(a, b, precision=HIGHEST, preferred_element_type=F32)


def as_row(x):
    return jnp.concatenate([x[t : t + 1, :] for t in range(x.shape[0])], axis=1)


def triangle(n):
    row = lax.broadcasted_iota(jnp.int32, (n, n), 0)
    col = lax.broadcasted_iota(jnp.int32, (n, n), 1)
    return row, col


def pack_symmetric(block):
    half = block.shape[0] // 2
    row, col = triangle(half)
    first, last = block[:half, :half], block[half:, half:]
    mixed = jnp.where(row >= col, first, last)
    diagonal = jnp.sum(jnp.where(row == col, last, 0.0), axis=0, keepdims=True)
    return block[half:, :half], mixed, diagonal


def unpack_symmetric(corner, mixed, diagonal):
    half = corner.shape[0]
    row, col = triangle(half)
    turned = mixed.T
    first = jnp.where(row >= col, mixed, turned)
    last = jnp.where(row < col, mixed, jnp.where(row == col, diagonal, turned))
    top = jnp.concatenate([first, corner.T], axis=1)
    return jnp.concatenate([top, jnp.concatenate([corner, last], axis=1)], axis=0)


def plan(boxes, samples, face):
    share = face // samples
    across = max(1, boxes * 8 // share)
    columns = 3 * face if across == 1 else 4 * face
    width = columns // across
    height = share * across // boxes
    return share, across, columns, width, height


def exchange_kernel(
    boxes, samples,
    operator_hbm, values_hbm, label_hbm, material_ref, permittivity_ref, slot_ref,
    left_hbm, through_hbm, other_hbm, interface_hbm, flux_hbm, scale_hbm, schur_hbm,
    total_hbm, residual_ref,
    left_ref, through_ref, other_ref, interface_ref, flux_ref, scale_ref, schur_ref,
    total_ref, stored, face_ref, values_ref, label_ref, loaded,
    rest, load, small, small_in, small_staged, small_final, large_in, large_staged, raw, partner,
    send_small, receive_small, send_large, receive_large,
    send_small_2, receive_small_2, send_large_2, receive_large_2,
    send_twin_small, receive_twin_small, send_twin, receive_twin,
):
    me = lax.axis_index("box")
    sample = lax.axis_index("mc")
    face, nodes = face_ref.shape
    outer = 3 * face
    half = face // 2
    results = [
        (left_ref, left_hbm), (through_ref, through_hbm), (other_ref, other_hbm),
        (interface_ref, interface_hbm), (flux_ref, flux_hbm), (scale_ref, scale_hbm),
        (schur_ref, schur_hbm), (total_ref, total_hbm),
    ]

    def store(index, cut=None):
        source, target = results[index]
        if cut is not None:
            source, target = source.at[cut], target.at[cut]
        pltpu.make_async_copy(source, target, stored.at[index]).start()

    share, across, columns, width, height = plan(boxes, samples, face)
    strip = face // boxes
    corner_strip = share // boxes
    at_strip = -(-corner_strip // 8) * 8
    kept = small_staged.shape[1]
    shift = lambda k: lax.rem(me + k + boxes, boxes)
    target = lambda box: {"box": box, "mc": sample}
    MESH = pl.DeviceIdType.MESH

    loads = [
        pltpu.make_async_copy(operator_hbm.at[pl.ds(outer, face)], face_ref, loaded.at[0]),
        pltpu.make_async_copy(label_hbm, label_ref, loaded.at[1]),
        pltpu.make_async_copy(values_hbm, values_ref, loaded.at[2]),
    ]
    for copy in loads:
        copy.start()
    rest_copy = pltpu.make_async_copy(operator_hbm.at[pl.ds(0, outer)], rest, load)
    rest_copy.start()
    barrier = pltpu.get_barrier_semaphore()

    def greet(k, carry):
        pl.semaphore_signal(barrier, inc=1, device_id=target(shift(k)), device_id_type=MESH)
        return carry

    lax.fori_loop(1, boxes, greet, 0)
    twins = [lax.rem(sample + t, samples) for t in range(1, samples)]
    for twin in twins:
        pl.semaphore_signal(
            barrier, inc=1, device_id={"box": me, "mc": twin}, device_id_type=MESH
        )

    def offset(i):
        step = (i + 1) // 2
        return boxes // 2 + jnp.where(lax.rem(i, 2) == 0, step, -step)

    halves = len(large_in)
    narrow = width // halves

    def piece(ref, group, j, part):
        row = group * share + (j // across) * height
        column = lax.rem(j, across) * width + part * narrow
        return ref.at[
            pl.ds(pl.multiple_of(row, 8), height),
            pl.ds(pl.multiple_of(column, 128), narrow),
        ]

    def send_all(source, landing, send, receive):
        def body(i, carry):
            k = offset(i)
            box = shift(k)
            pltpu.make_async_remote_copy(
                src_ref=source(box), dst_ref=landing, send_sem=send, recv_sem=receive(k),
                device_id=target(box), device_id_type=MESH,
            ).start()
            return carry

        lax.fori_loop(0, boxes - 1, body, 0)

    def drain(buffer, semaphore):
        pltpu.make_async_copy(buffer, buffer, semaphore).wait()

    others = pl.ds(0, boxes - 1)

    def send_part(part):
        send_all(
            lambda b: piece(face_ref, sample, b, part), large_in[part].at[me],
            send_large.at[part], lambda k: receive_large.at[part],
        )
        large_in[part][me] = piece(face_ref, sample, me, part)[...]

    loads[0].wait()
    pl.semaphore_wait(barrier, boxes - 1 + samples - 1)
    send_part(0)
    loads[1].wait()
    loads[2].wait()

    label = label_ref[...]
    level = jnp.zeros_like(label)
    for w in range(material_ref.shape[0]):
        level = jnp.where(label == w, material_ref[w], level)
    eps = jnp.zeros(label.shape, F32)
    for l in range(permittivity_ref.shape[0]):
        eps = jnp.where(level == l, permittivity_ref[l], eps)
    root = jnp.sqrt(eps)
    scale = as_row(root)
    scale_ref[...] = scale
    column = column_of(scale[:, outer:])
    own = face_ref[:, :outer] * widen(column, outer) * scale[:, :outer]
    own_parts = split(own)
    product = dot_split(own_parts, split(values_ref[...]))
    total_ref[...] = product

    square = face_ref[:, outer:]
    square = 0.5 * (square + square.T)
    corner, mixed, diagonal = pack_symmetric(square)
    mid = root.shape[1] // 2
    row_id = lax.broadcasted_iota(jnp.int32, root.shape, 0)
    lane_id = lax.broadcasted_iota(jnp.int32, root.shape, 1)
    turned = jnp.concatenate([diagonal[:, mid:], diagonal[:, :mid]], axis=1)
    extra = exact_dot(root, group_ends(2 * mid, False))
    extra = jnp.where((lane_id >= mid) & (row_id == 0), turned, extra)
    extra = jnp.where((lane_id >= mid) & (row_id == 1), diagonal, extra)
    packed = jnp.concatenate([corner, mixed], axis=0)
    mine = packed[:share]
    for group in range(1, samples):
        mine = jnp.where(sample == group, packed[group * share : (group + 1) * share], mine)
    for j in range(boxes):
        small[j, :corner_strip, :] = mine[j * corner_strip : (j + 1) * corner_strip, :]
        small[j, at_strip : at_strip + strip, :] = product[j * strip : (j + 1) * strip, :]
    small[:, kept:, :] = jnp.broadcast_to(extra[None], (boxes,) + extra.shape)
    schur_ref[...] = square * widen(column, face) * scale[:, outer:]

    send_all(lambda b: small.at[b], small_in.at[me], send_small, lambda k: receive_small)
    small_in[me] = small[me]
    for part in range(1, halves):
        send_part(part)
    store(5)

    def find(p, carry):
        wanted = slot_ref[p] ^ 1
        partner[p] = lax.fori_loop(
            0, boxes, lambda i, at: jnp.where(slot_ref[i] == wanted, i, at), jnp.int32(0)
        )
        return carry

    lax.fori_loop(0, boxes, find, 0)

    rest_copy.wait()
    values_parts = split(values_ref[...])
    for at in range(0, outer, face):
        cut = slice(at, at + face)
        rest[cut, :] = rest[cut, :] * widen(column_of(scale[:, cut]), nodes) * scale
        flux_ref[cut, :] = dot_split(split(rest[cut, :outer]), values_parts)

    drain(small_in.at[others], receive_small)

    def stage_small(p, carry):
        small_staged[p] = small_in[partner[p], 0:kept, :]
        return carry

    lax.fori_loop(0, boxes, stage_small, 0)
    send_all(
        lambda b: small_staged.at[b], small_final.at[sample, me], send_small_2,
        lambda k: receive_small_2.at[k],
    )
    small_final[sample, me] = small_staged[me]

    for part in range(halves):
        drain(large_in[part].at[others], receive_large.at[part])

        def stage_large(p, carry):
            large_staged[part, p] = large_in[part][partner[p]]
            return carry

        lax.fori_loop(0, boxes, stage_large, 0)
        send_all(
            lambda b: large_staged.at[part, b], piece(raw, sample, me, part),
            send_large_2.at[part], lambda k: receive_large_2.at[part, k],
        )
        piece(raw, sample, me, part)[...] = large_staged[part, me]

    def forward(block, send, receive):
        for t, twin in enumerate(twins):
            pltpu.make_async_remote_copy(
                src_ref=block, dst_ref=block, send_sem=send.at[t], recv_sem=receive.at[t],
                device_id={"box": me, "mc": twin}, device_id_type=MESH,
            ).start()

    small_part = lambda group, j: small_final.at[group, j, pl.ds(0, at_strip)]
    forward(small_part(sample, me), send_twin_small, receive_twin_small)

    def pass_small(i, carry):
        k = offset(i)
        source = shift(-k)
        drain(small_final.at[sample, source], receive_small_2.at[k])
        forward(small_part(sample, source), send_twin_small, receive_twin_small)
        return carry

    lax.fori_loop(0, boxes - 1, pass_small, 0)
    extra = small_in[partner[me], kept:, :]
    other_scale = as_row(exact_dot(extra, group_ends(2 * mid, True)))
    diagonal = jnp.concatenate([extra[0:1, mid:], extra[1:2, mid:]], axis=1)
    other_column = column_of(other_scale[:, outer:])
    for j in range(boxes):
        total_ref[j * strip : (j + 1) * strip, :] += small_final[
            sample, j, at_strip : at_strip + strip, :
        ]
    for t in range(samples - 1):
        origin = lax.rem(sample + samples - (t + 1), samples)
        drain(small_final.at[origin, :, pl.ds(0, at_strip)], receive_twin_small.at[t])
    pieces = [
        small_final[group, j, :corner_strip, :]
        for group in range(samples) for j in range(boxes)
    ]
    packed = jnp.concatenate(pieces, axis=0)
    square = unpack_symmetric(packed[:half], packed[half:], diagonal)
    schur_ref[...] += square * widen(other_column, face) * other_scale[:, outer:]

    for part in range(halves):
        forward(piece(raw, sample, me, part), send_twin, receive_twin)

    def pass_large(part):
        def body(i, carry):
            k = offset(i)
            source = shift(-k)
            drain(piece(raw, sample, source, part), receive_large_2.at[part, k])
            forward(piece(raw, sample, source, part), send_twin, receive_twin)
            return carry

        return body

    def work():
        store(6)
        store(7)
        schur = schur_ref[...]
        inverse_root = lax.rsqrt(jnp.sum(schur * eye(face), axis=0, keepdims=True))
        weights = widen(column_of(inverse_root), face) * inverse_root
        for result in fixed_inverse(schur * weights):
            if result is None:
                yield
        x, size = result
        residual_ref[0, 0] = size
        inverse = split(x * weights)
        total = split(total_ref[...])
        interface_ref[...] = -dot_split(inverse, total)
        store(3)
        yield
        for at in range(0, outer, face):
            cut = slice(at, at + face)
            through = dot_split(split(rest[cut, outer:]), inverse)
            through_ref[cut, :] = through
            through = split(through)
            flux_ref[cut, :] -= dot_split(through, total)
            store(1, cut)
            store(4, cut)
            yield
            left_ref[cut, :] = rest[cut, :outer] - dot_split(through, own_parts)
            store(0, cut)
            yield

    parts = 12
    steps = [(part, i) for part in range(halves) for i in range(boxes - 1)]

    def pass_steps(first, last):
        for part in range(halves):
            mine = [i for p, i in steps[first:last] if p == part]
            if mine:
                lax.fori_loop(mine[0], mine[-1] + 1, pass_large(part), 0)

    done = 0
    for count, _ in enumerate(work()):
        upto = min(len(steps), (count + 1) * len(steps) // parts)
        pass_steps(done, upto)
        done = upto
    pass_steps(done, len(steps))

    rows_of = lambda ref, group: ref.at[pl.ds(pl.multiple_of(group * share, 8), share)]
    for t in range(samples - 1):
        origin = lax.rem(sample + samples - (t + 1), samples)
        drain(rows_of(raw, origin), receive_twin.at[t])
    other_ref[...] = raw[:, :outer] * widen(other_column, outer) * other_scale[:, :outer]
    store(2)

    drain(small.at[others], send_small)
    for part in range(halves):
        drain(large_in[part].at[others], send_large.at[part])
        drain(large_staged.at[part, others], send_large_2.at[part])
    drain(small_staged.at[others], send_small_2)
    for t in range(samples - 1):
        drain(small_final.at[sample, :, pl.ds(0, at_strip)], send_twin_small.at[t])
        drain(rows_of(raw, sample), send_twin.at[t])
    for index, (source, target) in enumerate(results):
        pltpu.make_async_copy(source, target, stored.at[index]).wait()


def exchange(operator, values, label, material, permittivity, slot):
    boxes = lax.axis_size("box")
    samples = lax.axis_size("mc")
    nodes = operator.shape[1]
    face = nodes // 4
    outer = 3 * face
    count = values.shape[1]
    label = label.reshape(nodes // 128, 128)
    share, across, columns, width, height = plan(boxes, samples, face)
    kept = -(-(share // boxes) // 8) * 8 + -(-(face // boxes) // 8) * 8
    halves = 2 if width % 256 == 0 else (3 if width % 384 == 0 else 1)
    held = pl.BlockSpec(memory_space=pltpu.HBM)
    scalars = pl.BlockSpec(memory_space=pltpu.SMEM)
    dma = pltpu.SemaphoreType.DMA
    shapes = [
        (outer, outer), (outer, face), (face, outer), (face, count), (outer, count),
        (1, nodes), (face, face), (face, count),
    ]
    return pl.pallas_call(
        functools.partial(exchange_kernel, boxes, samples),
        in_specs=[held, held, held, scalars, scalars, scalars],
        out_specs=[pl.BlockSpec(memory_space=pl.ANY)] * len(shapes) + [scalars],
        out_shape=[jax.ShapeDtypeStruct(shape, F32) for shape in shapes + [(1, 1)]],
        scratch_shapes=[pltpu.VMEM(shape, F32) for shape in shapes] + [
            dma((len(shapes),)),
            pltpu.VMEM((face, nodes), F32),
            pltpu.VMEM(values.shape, F32),
            pltpu.VMEM(label.shape, jnp.int32),
            dma((3,)),
            pltpu.VMEM((outer, nodes), F32),
            dma,
            pltpu.VMEM((boxes, kept + nodes // 128, 128), F32),
            pltpu.VMEM((boxes, kept + nodes // 128, 128), F32),
            pltpu.VMEM((boxes, kept, 128), F32),
            pltpu.VMEM((samples, boxes, kept, 128), F32),
            (pltpu.VMEM((boxes, height, width // halves), F32),) * halves,
            pltpu.VMEM((halves, boxes, height, width // halves), F32),
            pltpu.VMEM((face, columns), F32),
            pltpu.SMEM((boxes,), jnp.int32),
            dma, dma, dma((halves,)), dma((halves,)),
            dma, dma((boxes,)), dma((halves,)), dma((halves, boxes)),
            dma((max(1, samples - 1),)), dma((max(1, samples - 1),)),
            dma((max(1, samples - 1),)), dma((max(1, samples - 1),)),
        ],
        compiler_params=pltpu.CompilerParams(
            collective_id=0, has_side_effects=True, vmem_limit_bytes=60 * 2**20
        ),
        name="exchange",
    )(operator, values, label, material, permittivity, slot)


def per_device(
    base_operator, exterior_values, wire_label, wire_material, permittivity, morton_slot
):
    parts = exchange(
        base_operator, exterior_values, wire_label, wire_material, permittivity, morton_slot
    )
    left, through, other, interface, flux, scale, schur, product, residual = parts
    return tuple(
        finish(
            left, through, other, interface, flux, residual,
            base_operator, exterior_values, scale, schur, product,
        )
    )


def solution(mesh):
    return jax.shard_map(
        per_device,
        mesh=mesh,
        in_specs=(P("box", None), P("box", None), P("box", None), P(), P("mc"), P()),
        out_specs=(P(("mc", "box"), None), P(("mc", "box"), None), P(("mc", "box"), None)),
        check_vma=False,
    )
```

```python
import functools

import jax
import jax.numpy as jnp
from jax import lax
from jax.experimental import pallas as pl
from jax.experimental.pallas import tpu as pltpu
from jax.sharding import PartitionSpec as P

F32 = jnp.float32
HIGHEST = lax.Precision.HIGHEST


def split(x):
    high = x.astype(jnp.bfloat16)
    low = (x - high.astype(F32)).astype(jnp.bfloat16)
    return high, low


def dot_split(a, b):
    (ah, al), (bh, bl) = a, b
    dot = functools.partial(jnp.dot, preferred_element_type=F32)
    return dot(ah, bh) + (dot(ah, bl) + dot(al, bh))


def dot3(a, b):
    return dot_split(split(a), split(b))


def column_of(row):
    return jnp.broadcast_to(row, (128, row.shape[1])).T


def widen(column, width):
    return jnp.concatenate([column] * (width // 128), axis=1)


def norm(x):
    return jnp.sqrt(jnp.sum(x * x))


def eye(n):
    row = lax.broadcasted_iota(jnp.int32, (n, n), 0)
    col = lax.broadcasted_iota(jnp.int32, (n, n), 1)
    return jnp.where(row == col, 1.0, 0.0).astype(F32)


def direct_inverse(s_ref, x_ref):
    n = s_ref.shape[0]
    x_ref[...] = s_ref[...]
    row_id = lax.broadcasted_iota(jnp.int32, (n, n), 0)
    col_id = lax.broadcasted_iota(jnp.int32, (n, n), 1)

    def step(k, carry):
        x = x_ref[...]
        on_row = row_id == k
        on_col = col_id == k
        row = jnp.sum(jnp.where(on_row, x, 0.0), axis=0, keepdims=True)
        col = jnp.sum(jnp.where(on_col, x, 0.0), axis=1, keepdims=True)
        pivot = jnp.sum(jnp.where(on_row & on_col, x, 0.0))
        scaled = row / pivot
        rest = x - col * scaled
        x = jnp.where(on_row, scaled, jnp.where(on_col, -col / pivot, rest))
        x_ref[...] = jnp.where(on_row & on_col, 1.0 / pivot, x)
        return carry

    lax.fori_loop(0, n, step, 0)


def invert(s_ref, x_ref, r_ref):
    s = s_ref[...]
    n = s.shape[0]
    unit = eye(n)
    alpha = n / jnp.sum(s * s)

    def begin(alpha):
        first = unit - alpha * s
        x_ref[...] = alpha * (unit + first)
        residual = dot3(first, first)
        r_ref[...] = residual
        return norm(residual)

    size = begin(alpha)

    def safe_start(_):
        return begin(1.0 / jnp.max(jnp.sum(jnp.abs(s), axis=0, keepdims=True)))

    size = lax.cond(size < 0.9, lambda size: size, safe_start, size)
    s_parts = split(s)

    def going(state):
        size, count = state
        return (size > 1e-2) & (count < 40)

    def improve(state):
        size, count = state
        x = x_ref[...]
        x = x + dot3(x, r_ref[...])
        x_ref[...] = x
        residual = unit - dot_split(s_parts, split(x))
        r_ref[...] = residual
        return norm(residual), count + 1

    size, _ = lax.while_loop(going, improve, (size, jnp.int32(0)))
    x = x_ref[...]
    x = x + dot3(x, r_ref[...])
    residual = unit - jnp.dot(s, x, precision=HIGHEST, preferred_element_type=F32)
    x_ref[...] = x + dot3(x, residual)
    converged = (size < 1e-2) & (norm(residual) < 1e-3)

    @pl.when(jnp.logical_not(converged))
    def _():
        direct_inverse(s_ref, x_ref)


def fixed_inverse(s):
    n = s.shape[0]
    unit = eye(n)
    alpha = n / jnp.sum(s * s)
    first = unit - alpha * s
    parts = split(s)
    x = alpha * (unit + first)
    residual = dot3(first, first)
    yield None
    x = x + dot3(x, residual)
    yield None
    residual = unit - dot_split(parts, split(x))
    yield None
    x = x + dot3(x, residual)
    yield None
    residual = unit - exact_dot(s, x)
    yield None
    yield x + dot3(x, residual), norm(residual)


def finish_kernel(
    left_ref, through_ref, other_ref, interface_in, flux_in, residual_ref,
    operator_ref, values_ref, scale_ref, schur_ref, product_ref,
    merged_ref, interface_ref, flux_ref,
    other_high, other_low, solved_high, solved_low, rows, s_ref, x_ref, r_ref, column_ref,
    values, schur, product, semaphore,
):
    block = left_ref.shape[0]
    face, outer = other_ref.shape
    step = pl.program_id(0)
    fast = residual_ref[0, 0] < 1e-3

    @pl.when(fast)
    def _():
        @pl.when(step == 0)
        def _():
            high, low = split(other_ref[...])
            other_high[...] = high
            other_low[...] = low
            interface_ref[...] = interface_in[...]

        merged_ref[:, :outer] = left_ref[...]
        through = split(through_ref[...])
        merged_ref[:, outer:] = -dot_split(through, (other_high[...], other_low[...]))
        flux_ref[...] = flux_in[...]

    def fetch(source, target):
        copy = pltpu.make_async_copy(source, target, semaphore)
        copy.start()
        copy.wait()

    @pl.when(jnp.logical_not(fast))
    def _():
        scale = scale_ref[...]

        @pl.when(step == 0)
        def _():
            column_ref[...] = column_of(scale)
            fetch(operator_ref.at[pl.ds(outer, face)], rows)
            fetch(values_ref, values)
            fetch(schur_ref, schur)
            fetch(product_ref, product)
            own = rows[:, :outer] * widen(column_ref[outer:, :], outer) * scale[:, :outer]
            s = schur[...]
            inverse_root = lax.rsqrt(jnp.sum(s * eye(face), axis=0, keepdims=True))
            root_column = column_of(inverse_root)
            s_ref[...] = s * inverse_root * widen(root_column, face)
            invert(s_ref, x_ref, r_ref)
            x = split(x_ref[...])

            def solve(right, at):
                width = right.shape[1]
                weights = widen(root_column, width)
                solved = dot_split(x, split(right * weights)) * weights
                high, low = split(solved)
                solved_high[:, at : at + width] = high
                solved_low[:, at : at + width] = low
                return solved

            solve(own, 0)
            solve(other_ref[...], outer)
            interface_ref[...] = -solve(product[...], 2 * outer)

        at = pl.multiple_of(step * block, block)
        fetch(operator_ref.at[pl.ds(at, block)], rows)
        mine = rows[...] * widen(column_ref[pl.ds(at, block), :], 4 * face) * scale
        across = split(mine[:, outer:])

        def apply(at, width):
            cut = slice(at, at + width)
            return dot_split(across, (solved_high[:, cut], solved_low[:, cut]))

        merged_ref[:, :outer] = mine[:, :outer] - apply(0, outer)
        merged_ref[:, outer:] = -apply(outer, outer)
        local = dot3(mine[:, :outer], values[...])
        flux_ref[...] = local - apply(2 * outer, flux_ref.shape[1])


def finish(left, through, other, interface, flux, residual, operator, values, scale, schur, product):
    outer = left.shape[0]
    face = outer // 3
    nodes = 4 * face
    count = values.shape[1]
    width = 2 * outer + count
    whole = lambda x: pl.BlockSpec(x.shape, lambda i: (0, 0))
    rows = lambda width: pl.BlockSpec((face, width), lambda i: (i, 0))
    anywhere = pl.BlockSpec(memory_space=pl.ANY)
    half = jnp.bfloat16
    return pl.pallas_call(
        finish_kernel,
        grid=(3,),
        in_specs=[
            rows(outer), rows(face), whole(other), whole(interface), rows(count),
            pl.BlockSpec(memory_space=pltpu.SMEM),
            anywhere, anywhere, whole(scale), anywhere, anywhere,
        ],
        out_specs=[rows(2 * outer), whole(interface), rows(count)],
        out_shape=[
            jax.ShapeDtypeStruct((outer, 2 * outer), F32),
            jax.ShapeDtypeStruct((face, count), F32),
            jax.ShapeDtypeStruct((outer, count), F32),
        ],
        scratch_shapes=[
            pltpu.VMEM((face, outer), half),
            pltpu.VMEM((face, outer), half),
            pltpu.VMEM((face, width), half),
            pltpu.VMEM((face, width), half),
            pltpu.VMEM((face, nodes), F32),
            pltpu.VMEM((face, face), F32),
            pltpu.VMEM((face, face), F32),
            pltpu.VMEM((face, face), F32),
            pltpu.VMEM((nodes, 128), F32),
            pltpu.VMEM((outer, count), F32),
            pltpu.VMEM((face, face), F32),
            pltpu.VMEM((face, count), F32),
            pltpu.SemaphoreType.DMA,
        ],
        compiler_params=pltpu.CompilerParams(vmem_limit_bytes=60 * 2**20),
        name="finish",
    )(left, through, other, interface, flux, residual, operator, values, scale, schur, product)


def group_ends(n, expand):
    row = lax.broadcasted_iota(jnp.int32, (n, n), 0)
    col = lax.broadcasted_iota(jnp.int32, (n, n), 1)
    take = (row < n // 2) & (col // 2 == row) if expand else (col < n // 2) & (row == 2 * col)
    return jnp.where(take, 1.0, 0.0).astype(F32)


def exact_dot(a, b):
    return jnp.dot(a, b, precision=HIGHEST, preferred_element_type=F32)


def as_row(x):
    return jnp.concatenate([x[t : t + 1, :] for t in range(x.shape[0])], axis=1)


def triangle(n):
    row = lax.broadcasted_iota(jnp.int32, (n, n), 0)
    col = lax.broadcasted_iota(jnp.int32, (n, n), 1)
    return row, col


def pack_symmetric(block):
    half = block.shape[0] // 2
    row, col = triangle(half)
    first, last = block[:half, :half], block[half:, half:]
    mixed = jnp.where(row >= col, first, last)
    diagonal = jnp.sum(jnp.where(row == col, last, 0.0), axis=0, keepdims=True)
    return block[half:, :half], mixed, diagonal


def unpack_symmetric(corner, mixed, diagonal):
    half = corner.shape[0]
    row, col = triangle(half)
    turned = mixed.T
    first = jnp.where(row >= col, mixed, turned)
    last = jnp.where(row < col, mixed, jnp.where(row == col, diagonal, turned))
    top = jnp.concatenate([first, corner.T], axis=1)
    return jnp.concatenate([top, jnp.concatenate([corner, last], axis=1)], axis=0)


def plan(boxes, samples, face):
    share = face // samples
    across = max(1, boxes * 8 // share)
    columns = 3 * face if across == 1 else 4 * face
    width = columns // across
    height = share * across // boxes
    return share, across, columns, width, height


def exchange_kernel(
    boxes, samples,
    operator_hbm, values_hbm, label_hbm, material_ref, permittivity_ref, slot_ref,
    left_hbm, through_hbm, other_hbm, interface_hbm, flux_hbm, scale_hbm, schur_hbm,
    total_hbm, residual_ref,
    left_ref, through_ref, other_ref, interface_ref, flux_ref, scale_ref, schur_ref,
    total_ref, stored, face_ref, values_ref, label_ref, loaded,
    rest, load, small, small_in, small_staged, small_final, large_in, large_staged, raw, partner,
    send_small, receive_small, send_large, receive_large,
    send_small_2, receive_small_2, send_large_2, receive_large_2,
    send_twin_small, receive_twin_small, send_twin, receive_twin,
):
    me = lax.axis_index("box")
    sample = lax.axis_index("mc")
    face, nodes = face_ref.shape
    outer = 3 * face
    half = face // 2
    results = [
        (left_ref, left_hbm), (through_ref, through_hbm), (other_ref, other_hbm),
        (interface_ref, interface_hbm), (flux_ref, flux_hbm), (scale_ref, scale_hbm),
        (schur_ref, schur_hbm), (total_ref, total_hbm),
    ]

    def store(index, cut=None):
        source, target = results[index]
        if cut is not None:
            source, target = source.at[cut], target.at[cut]
        pltpu.make_async_copy(source, target, stored.at[index]).start()

    share, across, columns, width, height = plan(boxes, samples, face)
    strip = face // boxes
    corner_strip = share // boxes
    at_strip = -(-corner_strip // 8) * 8
    kept = small_staged.shape[1]
    shift = lambda k: lax.rem(me + k + boxes, boxes)
    target = lambda box: {"box": box, "mc": sample}
    MESH = pl.DeviceIdType.MESH

    loads = [
        pltpu.make_async_copy(operator_hbm.at[pl.ds(outer, face)], face_ref, loaded.at[0]),
        pltpu.make_async_copy(label_hbm, label_ref, loaded.at[1]),
        pltpu.make_async_copy(values_hbm, values_ref, loaded.at[2]),
    ]
    for copy in loads:
        copy.start()
    rest_copy = pltpu.make_async_copy(operator_hbm.at[pl.ds(0, outer)], rest, load)
    rest_copy.start()
    barrier = pltpu.get_barrier_semaphore()

    def greet(k, carry):
        pl.semaphore_signal(barrier, inc=1, device_id=target(shift(k)), device_id_type=MESH)
        return carry

    lax.fori_loop(1, boxes, greet, 0)
    twins = [lax.rem(sample + t, samples) for t in range(1, samples)]
    for twin in twins:
        pl.semaphore_signal(
            barrier, inc=1, device_id={"box": me, "mc": twin}, device_id_type=MESH
        )

    def offset(i):
        step = (i + 1) // 2
        return boxes // 2 + jnp.where(lax.rem(i, 2) == 0, step, -step)

    halves = len(large_in)
    narrow = width // halves

    def piece(ref, group, j, part):
        row = group * share + (j // across) * height
        column = lax.rem(j, across) * width + part * narrow
        return ref.at[
            pl.ds(pl.multiple_of(row, 8), height),
            pl.ds(pl.multiple_of(column, 128), narrow),
        ]

    def send_all(source, landing, send, receive):
        def body(i, carry):
            k = offset(i)
            box = shift(k)
            pltpu.make_async_remote_copy(
                src_ref=source(box), dst_ref=landing, send_sem=send, recv_sem=receive(k),
                device_id=target(box), device_id_type=MESH,
            ).start()
            return carry

        lax.fori_loop(0, boxes - 1, body, 0)

    def drain(buffer, semaphore):
        pltpu.make_async_copy(buffer, buffer, semaphore).wait()

    others = pl.ds(0, boxes - 1)

    def send_part(part):
        send_all(
            lambda b: piece(face_ref, sample, b, part), large_in[part].at[me],
            send_large.at[part], lambda k: receive_large.at[part],
        )
        large_in[part][me] = piece(face_ref, sample, me, part)[...]

    loads[0].wait()
    pl.semaphore_wait(barrier, boxes - 1 + samples - 1)
    send_part(0)
    loads[1].wait()
    loads[2].wait()

    label = label_ref[...]
    level = jnp.zeros_like(label)
    for w in range(material_ref.shape[0]):
        level = jnp.where(label == w, material_ref[w], level)
    eps = jnp.zeros(label.shape, F32)
    for l in range(permittivity_ref.shape[0]):
        eps = jnp.where(level == l, permittivity_ref[l], eps)
    root = jnp.sqrt(eps)
    scale = as_row(root)
    scale_ref[...] = scale
    column = column_of(scale[:, outer:])
    own = face_ref[:, :outer] * widen(column, outer) * scale[:, :outer]
    own_parts = split(own)
    product = dot_split(own_parts, split(values_ref[...]))
    total_ref[...] = product

    square = face_ref[:, outer:]
    square = 0.5 * (square + square.T)
    corner, mixed, diagonal = pack_symmetric(square)
    mid = root.shape[1] // 2
    row_id = lax.broadcasted_iota(jnp.int32, root.shape, 0)
    lane_id = lax.broadcasted_iota(jnp.int32, root.shape, 1)
    turned = jnp.concatenate([diagonal[:, mid:], diagonal[:, :mid]], axis=1)
    extra = exact_dot(root, group_ends(2 * mid, False))
    extra = jnp.where((lane_id >= mid) & (row_id == 0), turned, extra)
    extra = jnp.where((lane_id >= mid) & (row_id == 1), diagonal, extra)
    packed = jnp.concatenate([corner, mixed], axis=0)
    mine = packed[:share]
    for group in range(1, samples):
        mine = jnp.where(sample == group, packed[group * share : (group + 1) * share], mine)
    for j in range(boxes):
        small[j, :corner_strip, :] = mine[j * corner_strip : (j + 1) * corner_strip, :]
        small[j, at_strip : at_strip + strip, :] = product[j * strip : (j + 1) * strip, :]
    small[:, kept:, :] = jnp.broadcast_to(extra[None], (boxes,) + extra.shape)
    schur_ref[...] = square * widen(column, face) * scale[:, outer:]

    send_all(lambda b: small.at[b], small_in.at[me], send_small, lambda k: receive_small)
    small_in[me] = small[me]
    store(5)

    def find(p, carry):
        wanted = slot_ref[p] ^ 1
        partner[p] = lax.fori_loop(
            0, boxes, lambda i, at: jnp.where(slot_ref[i] == wanted, i, at), jnp.int32(0)
        )
        return carry

    lax.fori_loop(0, boxes, find, 0)

    rest_copy.wait()
    values_parts = split(values_ref[...])
    for at in range(0, outer, face):
        cut = slice(at, at + face)
        rest[cut, :] = rest[cut, :] * widen(column_of(scale[:, cut]), nodes) * scale
        flux_ref[cut, :] = dot_split(split(rest[cut, :outer]), values_parts)

    drain(small.at[others], send_small)
    for part in range(1, halves):
        send_part(part)
    drain(small_in.at[others], receive_small)

    def stage_small(p, carry):
        small_staged[p] = small_in[partner[p], 0:kept, :]
        return carry

    lax.fori_loop(0, boxes, stage_small, 0)
    send_all(
        lambda b: small_staged.at[b], small_final.at[sample, me], send_small_2,
        lambda k: receive_small_2.at[k],
    )
    small_final[sample, me] = small_staged[me]
    drain(small_staged.at[others], send_small_2)

    for part in range(halves):
        drain(large_in[part].at[others], receive_large.at[part])

        def stage_large(p, carry):
            large_staged[part, p] = large_in[part][partner[p]]
            return carry

        lax.fori_loop(0, boxes, stage_large, 0)
        send_all(
            lambda b: large_staged.at[part, b], piece(raw, sample, me, part),
            send_large_2.at[part], lambda k: receive_large_2.at[part, k],
        )
        piece(raw, sample, me, part)[...] = large_staged[part, me]

    def forward(block, send, receive):
        for t, twin in enumerate(twins):
            pltpu.make_async_remote_copy(
                src_ref=block, dst_ref=block, send_sem=send.at[t], recv_sem=receive.at[t],
                device_id={"box": me, "mc": twin}, device_id_type=MESH,
            ).start()

    small_part = lambda group, j: small_final.at[group, j, pl.ds(0, at_strip)]
    forward(small_part(sample, me), send_twin_small, receive_twin_small)

    def pass_small(i, carry):
        k = offset(i)
        source = shift(-k)
        drain(small_final.at[sample, source], receive_small_2.at[k])
        forward(small_part(sample, source), send_twin_small, receive_twin_small)
        return carry

    lax.fori_loop(0, boxes - 1, pass_small, 0)
    extra = small_in[partner[me], kept:, :]
    other_scale = as_row(exact_dot(extra, group_ends(2 * mid, True)))
    diagonal = jnp.concatenate([extra[0:1, mid:], extra[1:2, mid:]], axis=1)
    other_column = column_of(other_scale[:, outer:])
    for j in range(boxes):
        total_ref[j * strip : (j + 1) * strip, :] += small_final[
            sample, j, at_strip : at_strip + strip, :
        ]
    for t in range(samples - 1):
        origin = lax.rem(sample + samples - (t + 1), samples)
        drain(small_final.at[origin, :, pl.ds(0, at_strip)], receive_twin_small.at[t])
    pieces = [
        small_final[group, j, :corner_strip, :]
        for group in range(samples) for j in range(boxes)
    ]
    packed = jnp.concatenate(pieces, axis=0)
    square = unpack_symmetric(packed[:half], packed[half:], diagonal)
    schur_ref[...] += square * widen(other_column, face) * other_scale[:, outer:]

    for part in range(halves):
        forward(piece(raw, sample, me, part), send_twin, receive_twin)

    def pass_large(part):
        def body(i, carry):
            k = offset(i)
            source = shift(-k)
            drain(piece(raw, sample, source, part), receive_large_2.at[part, k])
            forward(piece(raw, sample, source, part), send_twin, receive_twin)
            return carry

        return body

    def work():
        store(6)
        store(7)
        schur = schur_ref[...]
        inverse_root = lax.rsqrt(jnp.sum(schur * eye(face), axis=0, keepdims=True))
        weights = widen(column_of(inverse_root), face) * inverse_root
        for result in fixed_inverse(schur * weights):
            if result is None:
                yield
        x, size = result
        residual_ref[0, 0] = size
        inverse = split(x * weights)
        total = split(total_ref[...])
        interface_ref[...] = -dot_split(inverse, total)
        store(3)
        yield
        for at in range(0, outer, face):
            cut = slice(at, at + face)
            through = dot_split(split(rest[cut, outer:]), inverse)
            through_ref[cut, :] = through
            through = split(through)
            flux_ref[cut, :] -= dot_split(through, total)
            store(1, cut)
            store(4, cut)
            yield
            left_ref[cut, :] = rest[cut, :outer] - dot_split(through, own_parts)
            store(0, cut)
            yield

    parts = 12
    steps = [(part, i) for part in range(halves) for i in range(boxes - 1)]

    def pass_steps(first, last):
        for part in range(halves):
            mine = [i for p, i in steps[first:last] if p == part]
            if mine:
                lax.fori_loop(mine[0], mine[-1] + 1, pass_large(part), 0)

    done = 0
    for count, _ in enumerate(work()):
        upto = min(len(steps), (count + 1) * len(steps) // parts)
        pass_steps(done, upto)
        done = upto
    pass_steps(done, len(steps))

    rows_of = lambda ref, group: ref.at[pl.ds(pl.multiple_of(group * share, 8), share)]
    for t in range(samples - 1):
        origin = lax.rem(sample + samples - (t + 1), samples)
        drain(rows_of(raw, origin), receive_twin.at[t])
    other_ref[...] = raw[:, :outer] * widen(other_column, outer) * other_scale[:, :outer]
    store(2)

    for part in range(halves):
        drain(large_in[part].at[others], send_large.at[part])
        drain(large_staged.at[part, others], send_large_2.at[part])
    for t in range(samples - 1):
        drain(small_final.at[sample, :, pl.ds(0, at_strip)], send_twin_small.at[t])
        drain(rows_of(raw, sample), send_twin.at[t])
    for index, (source, target) in enumerate(results):
        pltpu.make_async_copy(source, target, stored.at[index]).wait()


def exchange(operator, values, label, material, permittivity, slot):
    boxes = lax.axis_size("box")
    samples = lax.axis_size("mc")
    nodes = operator.shape[1]
    face = nodes // 4
    outer = 3 * face
    count = values.shape[1]
    label = label.reshape(nodes // 128, 128)
    share, across, columns, width, height = plan(boxes, samples, face)
    kept = -(-(share // boxes) // 8) * 8 + -(-(face // boxes) // 8) * 8
    halves = 2 if width % 256 == 0 else (3 if width % 384 == 0 else 1)
    held = pl.BlockSpec(memory_space=pltpu.HBM)
    scalars = pl.BlockSpec(memory_space=pltpu.SMEM)
    dma = pltpu.SemaphoreType.DMA
    shapes = [
        (outer, outer), (outer, face), (face, outer), (face, count), (outer, count),
        (1, nodes), (face, face), (face, count),
    ]
    return pl.pallas_call(
        functools.partial(exchange_kernel, boxes, samples),
        in_specs=[held, held, held, scalars, scalars, scalars],
        out_specs=[pl.BlockSpec(memory_space=pl.ANY)] * len(shapes) + [scalars],
        out_shape=[jax.ShapeDtypeStruct(shape, F32) for shape in shapes + [(1, 1)]],
        scratch_shapes=[pltpu.VMEM(shape, F32) for shape in shapes] + [
            dma((len(shapes),)),
            pltpu.VMEM((face, nodes), F32),
            pltpu.VMEM(values.shape, F32),
            pltpu.VMEM(label.shape, jnp.int32),
            dma((3,)),
            pltpu.VMEM((outer, nodes), F32),
            dma,
            pltpu.VMEM((boxes, kept + nodes // 128, 128), F32),
            pltpu.VMEM((boxes, kept + nodes // 128, 128), F32),
            pltpu.VMEM((boxes, kept, 128), F32),
            pltpu.VMEM((samples, boxes, kept, 128), F32),
            (pltpu.VMEM((boxes, height, width // halves), F32),) * halves,
            pltpu.VMEM((halves, boxes, height, width // halves), F32),
            pltpu.VMEM((face, columns), F32),
            pltpu.SMEM((boxes,), jnp.int32),
            dma, dma, dma((halves,)), dma((halves,)),
            dma, dma((boxes,)), dma((halves,)), dma((halves, boxes)),
            dma((max(1, samples - 1),)), dma((max(1, samples - 1),)),
            dma((max(1, samples - 1),)), dma((max(1, samples - 1),)),
        ],
        compiler_params=pltpu.CompilerParams(
            collective_id=0, has_side_effects=True, vmem_limit_bytes=60 * 2**20
        ),
        name="exchange",
    )(operator, values, label, material, permittivity, slot)


def per_device(
    base_operator, exterior_values, wire_label, wire_material, permittivity, morton_slot
):
    parts = exchange(
        base_operator, exterior_values, wire_label, wire_material, permittivity, morton_slot
    )
    left, through, other, interface, flux, scale, schur, product, residual = parts
    return tuple(
        finish(
            left, through, other, interface, flux, residual,
            base_operator, exterior_values, scale, schur, product,
        )
    )


def solution(mesh):
    return jax.shard_map(
        per_device,
        mesh=mesh,
        in_specs=(P("box", None), P("box", None), P("box", None), P(), P("mc"), P()),
        out_specs=(P(("mc", "box"), None), P(("mc", "box"), None), P(("mc", "box"), None)),
        check_vma=False,
    )
```
